256 devices in a mesh: slab: 32 (over z, x), pencil: 8 (over y, core).
Axes of the slice: x: 4, y: 4, z: 8, core: 2. Of those that a mesh axis runs over, the one named last changes fastest.
Arguments:
- vorticity: float32 [3, 256, 256, 256], P(None, 'slab', 'pencil')
- velocity: float32 [3, 256, 256, 256], P(None, 'slab', 'pencil'), may hold values from -6 to 6
- viscosity: float32 [256, 256, 256], P('slab', 'pencil'), may hold values from 0.02 to 0.4
- tile_weights: float32 [8192, 3, 128], P(('slab', 'pencil')), may hold values from -6 to 6
- tile_cells: int32 [8192, 128], P(('slab', 'pencil')), may hold values from 0 to 65535
- tile_dest: int32 [8192, 1], P(('slab', 'pencil')), may hold values from 0 to 31; in each aligned block of 32 rows (0 to 31, 32 to 63, ...) at most 2 rows name the same one
- tile_count: int32 [256], P(('slab', 'pencil')), may hold values from 8 to 32, as said below
Outputs:
- vorticity_out: float32 [3, 256, 256, 256], P(None, 'slab', 'pencil')
- far_velocity: float32 [3, 32, 8, 16], P(None, 'slab', 'pencil')
The draws below stay inside these ranges and needn't reach their ends.
Inputs may be any that keep to these rules, and one draw needn't show every extreme that they name: Tiles of device (s, p) go to device (tile_dest, p). Among the 32 tiles of one device, at most 2 name one slab, a bound that some block reaches. The live tiles of a device are its first tile_count ones; some device has all 32 live.
All inputs are finite; a program needn't handle non-finite values.
Results may differ from the reference program's by a relative error of at most 0.0003.
Values sent between devices are 32-bit elements; how exact they have to be, the bound alone decides.
A program may use at most 128 MiB of HBM per device.

```python
import math
import jax
import jax.numpy as jnp
import numpy as np
from jax import lax

CX = 8
CY = 32
NZ = 256
TILES = 32
CB = 16
TC = 128
NX = 256
NY = 256
CELLS = 65536
NCL = 16
CAP = 2
TILES_ALL = 8192
SIGMA = 64
N_SLAB = 32
N_PENCIL = 8


def draw_vorticity(key, part):
    first = jax.random.fold_in(key, 0)
    shape = (3, NX, NY, NZ)
    return jax.random.normal(first, shape, jnp.float32)


def draw_tile_count(key, part):
    first, second = jax.random.split(jax.random.fold_in(key, 7))
    devices_all = N_SLAB * N_PENCIL
    counts = jax.random.randint(first, (devices_all,), TILES // 4, TILES + 1, jnp.int32)
    chosen = jax.random.randint(second, (), 0, devices_all, jnp.int32)
    return counts.at[chosen].set(TILES)


def touch_ends(drawn, stream_key, low, largest):
    place = [jax.random.randint(jax.random.fold_in(stream_key, axis), (), 0, length) for axis, length in enumerate(drawn.shape)]
    widest = drawn.shape.index(max(drawn.shape))
    next_to = place[:widest] + [(place[widest] + 1) % drawn.shape[widest]] + place[widest + 1:]
    return drawn.at[tuple(place)].set(low).at[tuple(next_to)].set(largest)


def shard_levels(rng, extent, cuts, low, high):
    def one(axis_at, blocks):
        steps = jax.random.uniform(jax.random.fold_in(jax.random.fold_in(rng, 6), axis_at), (blocks,), jnp.float32, low / len(cuts), high / len(cuts))
        return jnp.repeat(jnp.exp(steps), extent[axis_at] // blocks).reshape((-1,) + (1,) * (len(extent) - axis_at - 1))

    gain = one(*cuts[0])
    for cut in cuts[1:]:
        gain = gain * one(*cut)
    return gain


def assign_block(stream_key, own, number, rows, amount, top, reach, slope):
    ranking = jax.random.permutation(stream_key, amount)
    crowded, ordinary = load_shares(amount, rows * top, reach, slope, True), load_shares(amount, rows * top, reach, slope, False)
    places = jnp.arange(amount)

    def named(lengths, turn):
        used = int((lengths > 0).sum())
        fixed = max(1, used // 4)
        passed = fixed + (places - fixed + turn * (used - fixed)) % max(1, amount - fixed)
        return jnp.zeros((amount,), jnp.int32).at[ranking[jnp.where(places < fixed, places, passed)]].set(jnp.asarray(lengths, jnp.int32))

    lengths = jnp.where(number % 4 == 0, named(crowded, number // 4), named(ordinary, number - number // 4 - 1))
    mixed = jax.random.permutation(jax.random.fold_in(own, 3), amount)
    donor, taker = mixed[0:amount // 2 * 2:2], mixed[1:amount // 2 * 2:2]
    margin = jnp.minimum(lengths[donor] - 1, reach - lengths[taker]) // 2
    margin = jnp.where((donor == ranking[0]) | (taker == ranking[0]) | (lengths[taker] == 0), 0, jnp.maximum(margin, 0))
    passed = jax.random.randint(jax.random.fold_in(own, 4), (amount // 2,), 0, 1 << 20) % (margin + 1)
    lengths = lengths.at[donor].add(-passed).at[taker].add(passed)
    labels = jnp.searchsorted(jnp.cumsum(lengths), jnp.arange(rows * top), side="right").astype(jnp.int32)
    grid = labels.reshape(top, rows).T
    grid = grid[jax.random.permutation(jax.random.fold_in(own, 1), rows)]
    turn = jax.random.randint(jax.random.fold_in(own, 2), (rows, 1), 0, top)
    return jnp.take_along_axis(grid, (jnp.arange(top)[None, :] + turn) % top, axis=1)


def load_shares(amount, total, limit, skew, full):
    weights = [(1 << 20) // math.isqrt(standing ** skew) + 1 for standing in range(1, amount + 1)]
    largest = limit if full else min(limit, max(-(-total // amount), total * weights[0] // sum(weights)))
    least = 1 if total - largest >= amount - 1 else 0
    holding, surplus = [largest] + [least] * (amount - 1), total - largest - least * (amount - 1)
    while surplus > 0:
        free = [i for i in range(1, amount) if holding[i] < largest] or [i for i in range(1, amount) if holding[i] < limit]
        mass, budget = sum([weights[i] for i in free]), surplus
        for i in free:
            more = min(limit - holding[i], max(1, budget * weights[i] // mass), surplus)
            holding[i] = holding[i] + more
            surplus = surplus - more
    return np.array(holding)


def bell_draw(own_key, shape, spread, limit, cuts=(), kind=jnp.bfloat16):
    result = jax.random.normal(own_key, shape, jnp.float32) * spread
    if len(cuts) > 0:
        result = shard_levels(own_key, shape, cuts, -0.22, 0.18) * result
    return jnp.clip(result, min=-limit, max=limit).astype(kind)


def setup_inputs(seed: int = 0) -> dict:
    key_of = jax.random.split(jax.random.key(seed), 8)
    vorticity = draw_vorticity(jax.random.fold_in(key_of[7], 71), 0)
    velocity = bell_draw(key_of[1], (3, NX, NY, NZ), 1.0, 6.0, ((1, 32), (2, 8)), jnp.float32)
    viscosity = jnp.clip(jnp.exp(math.log(0.4) - 2.9957323 * jax.random.uniform(key_of[2], (NX, NY, NZ), jnp.float32) ** shard_levels(key_of[2], (NX, NY, NZ), ((0, 32), (1, 8)), -0.2, 0.2)), 0.02, 0.4)
    tile_weights = bell_draw(key_of[3], (TILES_ALL, 3, TC), 1.0, 6.0, ((0, 256),), jnp.float32)
    tile_cells = touch_ends(jax.random.randint(key_of[4], (TILES_ALL, TC), 0, CELLS), jax.random.fold_in(key_of[4], 1), 0, CELLS - 1).astype(jnp.int32)
    tile_dest_keys = jax.random.split(jax.random.fold_in(key_of[5], 1), TILES_ALL // TILES)
    tile_dest_turns = jax.random.permutation(jax.random.fold_in(key_of[5], 3), TILES_ALL // TILES)
    tile_dest = jax.vmap(lambda own, number: assign_block(jax.random.fold_in(key_of[5], 2), own, number, TILES, N_SLAB, 1, CAP, 2))(tile_dest_keys, tile_dest_turns).reshape((TILES_ALL, 1))
    tile_count = draw_tile_count(jax.random.fold_in(key_of[7], 71), 0)
    return {"vorticity": vorticity, "velocity": velocity, "viscosity": viscosity, "tile_weights": tile_weights, "tile_cells": tile_cells, "tile_dest": tile_dest, "tile_count": tile_count}


time_step = 0.1

def interior(a):
    return a[..., 1:-1, 1:-1, :]

def ahead_x(a):
    return a[..., 2:, 1:-1, :]

def behind_x(a):
    return a[..., :-2, 1:-1, :]

def ahead_y(a):
    return a[..., 1:-1, 2:, :]

def behind_y(a):
    return a[..., 1:-1, :-2, :]

def ahead_z(a):
    return jnp.roll(interior(a), -1, axis=-1)

def behind_z(a):
    return jnp.roll(interior(a), 1, axis=-1)

def advance(padded):
    vort_all = padded[0:3]
    velo_all = padded[3:6]
    visc_all = padded[6]
    stencil_pairs = ((ahead_x, behind_x), (ahead_y, behind_y), (ahead_z, behind_z))
    own_vort = interior(vort_all)
    own_visc = interior(visc_all)
    stretch = jnp.zeros_like(own_vort)
    diffuse = jnp.zeros_like(own_vort)
    for axis_num in range(3):
        forward, backward = stencil_pairs[axis_num]
        stretch = stretch + own_vort[axis_num] * (0.5 * (forward(velo_all) - backward(velo_all)))
        for neighbour in stencil_pairs[axis_num]:
            diffuse = diffuse + 0.5 * (own_visc + neighbour(visc_all)) * (neighbour(vort_all) - own_vort)
    return own_vort + time_step * (stretch + diffuse)

def centres(cols, cx, cy, cb, npencil, ncl):
    slab_idx = cols // (npencil * ncl)
    pencil_idx = cols // ncl % npencil
    level = cols % ncl
    xpos = (slab_idx * cx).astype(jnp.float32) + (cx - 1) * 0.5
    ypos = (pencil_idx * cy).astype(jnp.float32) + (cy - 1) * 0.5
    zpos = (level * cb).astype(jnp.float32) + (cb - 1) * 0.5
    return (xpos, ypos, zpos)

def far_terms(targets, sources, moments, sigma):
    high = lax.Precision.HIGHEST
    rel_x = targets[0][:, None] - sources[0][None, :]
    rel_y = targets[1][:, None] - sources[1][None, :]
    rel_z = targets[2][:, None] - sources[2][None, :]
    dist_sq = rel_x * rel_x + rel_y * rel_y + rel_z * rel_z + sigma * sigma
    inverse = lax.rsqrt(dist_sq)
    weight = inverse * inverse * inverse
    trans = moments.T
    along_x = jnp.dot(weight * rel_x, trans, precision=high)
    along_y = jnp.dot(weight * rel_y, trans, precision=high)
    along_z = jnp.dot(weight * rel_z, trans, precision=high)
    first = along_z[:, 1] - along_y[:, 2]
    second = along_x[:, 2] - along_z[:, 0]
    third = along_y[:, 0] - along_x[:, 1]
    return jnp.stack([first, second, third], 0)

def reference(vorticity, velocity, viscosity, tile_weights, tile_cells, tile_dest, tile_count):
    stacked = jnp.concatenate([vorticity, velocity, viscosity[None]], 0)
    padded = jnp.pad(stacked, ((0, 0), (1, 1), (1, 1), (0, 0)))
    advanced = advance(padded)
    rows = jnp.arange(TILES_ALL, dtype=jnp.int32)
    device = rows // TILES
    pencil_idx = device % N_PENCIL
    live = (rows % TILES < tile_count[device]).astype(jnp.float32)
    cells = tile_cells
    local_x = cells // (CY * NZ)
    local_y = cells // NZ % CY
    local_z = cells % NZ
    grid_x = tile_dest[:, 0:1] * CX + local_x
    grid_y = pencil_idx[:, None] * CY + local_y
    flat = ((grid_x * NY + grid_y) * NZ + local_z).astype(jnp.int32)
    values = tile_weights * live[:, None, None]
    values = jnp.transpose(values, (1, 0, 2)).reshape(3, -1)
    field = advanced.reshape(3, NX * NY * NZ)
    field = field.at[:, flat.reshape(-1)].add(values)
    vorticity_out = field.reshape(3, NX, NY, NZ)
    moment = vorticity_out.reshape(3, N_SLAB, CX, N_PENCIL, CY, NCL, CB).sum(axis=(2, 4, 6))
    moment = moment.reshape(3, N_SLAB * N_PENCIL * NCL)
    all_cols = jnp.arange(N_SLAB * N_PENCIL * NCL, dtype=jnp.int32)
    sources = centres(all_cols, CX, CY, CB, N_PENCIL, NCL)
    sigma = jnp.float32(SIGMA)

    def per_device(dev):
        cols = dev * NCL + jnp.arange(NCL, dtype=jnp.int32)
        return far_terms(centres(cols, CX, CY, CB, N_PENCIL, NCL), sources, moment, sigma)
    blocks = lax.map(per_device, jnp.arange(N_SLAB * N_PENCIL, dtype=jnp.int32))
    far_velocity = jnp.transpose(blocks, (1, 0, 2)).reshape(3, N_SLAB, N_PENCIL, NCL)
    return (vorticity_out, far_velocity)
```

```python
import functools

import jax
import jax.numpy as jnp
from jax import lax
from jax.experimental import pallas as pl
from jax.experimental.pallas import tpu as pltpu
from jax.sharding import PartitionSpec as P

CB = 16
FIELDS = 7
time_step = 0.1
HIGH = lax.Precision.HIGHEST
F32 = jnp.float32
BF16 = jnp.bfloat16
MESH = pl.DeviceIdType.MESH


def iota(shape, dim):
    return lax.broadcasted_iota(jnp.int32, shape, dim)


def signal_peers(axis, me, count, offsets):
    barrier = pltpu.get_barrier_semaphore()

    def one(k, carry):
        peer = lax.rem(me + k, count)
        pl.semaphore_signal(barrier, inc=1, device_id={axis: peer}, device_id_type=MESH)
        return carry

    lax.fori_loop(offsets[0], offsets[1], one, 0)


def remote(src, dst, send_sem, recv_sem, device):
    return pltpu.make_async_remote_copy(
        src_ref=src, dst_ref=dst, send_sem=send_sem, recv_sem=recv_sem, device_id=device, device_id_type=MESH
    )


def pack_tiles(weights, cells, dest, live, send, n_slab):
    tiles = cells.shape[0]
    slab = iota((n_slab, tiles), 0)
    tile = iota((n_slab, tiles), 1)
    match = jnp.where((dest[...] == slab) & (tile < live), 1.0, 0.0)
    earlier = jnp.where(iota((tiles, tiles), 0) < iota((tiles, tiles), 1), 1.0, 0.0)
    before = jnp.dot(match, earlier, preferred_element_type=F32)
    for j in range(2):
        pick = jnp.where(before == j, match, 0.0)
        for c in range(4):
            rows = weights[c] if c < 3 else (cells[...] + 1).astype(F32)
            send[:, 4 * j + c, :] = jnp.dot(pick, rows, precision=HIGH, preferred_element_type=F32)


def exchange_kernel(
    n_slab, n_pencil, vort, velo, visc, weights, cells, dest, count,
    tiles, xhalo, yhalo, field, send, yface, load_sem, xsend, xrecv, ysend, yrecv, tsend, trecv,
):
    slab, pencil = lax.axis_index("slab"), lax.axis_index("pencil")
    cx, cy = field.shape[1], field.shape[2]
    barrier = pltpu.get_barrier_semaphore()
    signal_peers("slab", slab, n_slab, (1, n_slab))
    p_up, p_down = lax.rem(pencil + 1, n_pencil), lax.rem(pencil + n_pencil - 1, n_pencil)
    for peer in (p_up, p_down):
        pl.semaphore_signal(barrier, inc=1, device_id={"pencil": peer}, device_id_type=MESH)
    loads = [
        pltpu.make_async_copy(vort, field.at[0:3], load_sem.at[0]),
        pltpu.make_async_copy(velo, field.at[3:6], load_sem.at[1]),
        pltpu.make_async_copy(visc, field.at[6], load_sem.at[2]),
    ]
    for load in loads:
        load.start()
    pack_tiles(weights, cells, dest, count[0], send, n_slab)
    for load in loads:
        load.wait()
    for c in range(FIELDS):
        yface[0, c] = field[c, :, 0, :]
        yface[1, c] = field[c, :, cy - 1, :]
    pl.semaphore_wait(barrier, n_slab - 1 + 2)

    s_up, s_down = lax.rem(slab + 1, n_slab), lax.rem(slab + n_slab - 1, n_slab)
    halos = [
        remote(field.at[:, 0], xhalo.at[1], xsend.at[0], xrecv.at[1], {"slab": s_down}),
        remote(field.at[:, cx - 1], xhalo.at[0], xsend.at[1], xrecv.at[0], {"slab": s_up}),
        remote(yface.at[0], yhalo.at[1], ysend.at[0], yrecv.at[1], {"pencil": p_down}),
        remote(yface.at[1], yhalo.at[0], ysend.at[1], yrecv.at[0], {"pencil": p_up}),
    ]
    for halo in halos:
        halo.start()

    def deliver(k, carry):
        peer = lax.rem(slab + k, n_slab)
        remote(send.at[peer], tiles.at[k], tsend, trecv, {"slab": peer}).start()
        return carry

    lax.fori_loop(1, n_slab, deliver, 0)
    tiles[0] = send[slab]
    everything = remote(send.at[1:n_slab], tiles.at[1:n_slab], tsend, trecv, {"slab": s_up})
    everything.wait_send()
    everything.wait_recv()
    for halo in halos:
        halo.wait()


def deposit(tiles, lhs, rhs, total):
    rows, nz = total.shape[0] // 3, total.shape[1]
    width = 2 * tiles.shape[2]
    shift = nz.bit_length() - 1
    number = iota((rows, width), 0).astype(F32).astype(BF16)
    total[...] = jnp.zeros_like(total)

    def add(i, carry):
        tile = tiles[i]
        entry = [jnp.concatenate([tile[c : c + 1], tile[4 + c : 5 + c]], axis=1) for c in range(4)]
        cell = entry[3].astype(jnp.int32) - 1
        high = (cell >> shift).astype(F32).astype(BF16)
        low = (cell & (nz - 1)).astype(F32).astype(BF16)
        here = number == high
        for c in range(3):
            first = entry[c].astype(BF16)
            second = (entry[c] - first.astype(F32)).astype(BF16)
            lhs[c * rows : (c + 1) * rows, 0:width] = jnp.where(here, first, jnp.zeros_like(first))
            lhs[c * rows : (c + 1) * rows, width : 2 * width] = jnp.where(here, second, jnp.zeros_like(second))
        onehot = jnp.where(number == low, jnp.ones((), BF16), jnp.zeros((), BF16))
        rhs[:, 0:width] = onehot
        rhs[:, width : 2 * width] = onehot
        total[...] += lax.dot_general(
            lhs[...], rhs[...], (((1,), (1,)), ((), ())), preferred_element_type=F32
        )
        return carry

    lax.fori_loop(0, tiles.shape[0], add, 0)


def block_kernel(
    n_slab, n_pencil, vort, velo, visc, xhalo, yhalo, tiles, out, moment, field, lhs, rhs, total, load_sem
):
    slab, pencil = lax.axis_index("slab"), lax.axis_index("pencil")
    cx, cy, nz = out.shape[1], out.shape[2], out.shape[3]
    loads = [
        pltpu.make_async_copy(vort, field.at[0:3, 1 : cx + 1], load_sem.at[0]),
        pltpu.make_async_copy(velo, field.at[3:6, 1 : cx + 1], load_sem.at[1]),
        pltpu.make_async_copy(visc, field.at[6, 1 : cx + 1], load_sem.at[2]),
    ]
    for load in loads:
        load.start()
    field[:, 0] = jnp.where(slab > 0, xhalo[0], 0.0)
    field[:, cx + 1] = jnp.where(slab < n_slab - 1, xhalo[1], 0.0)
    deposit(tiles, lhs, rhs, total)
    for load in loads:
        load.wait()
    row = iota((cy, nz), 0)
    first_row, last_row = row == 0, row == cy - 1
    has_before, has_after = pencil > 0, pencil < n_pencil - 1

    def plane(x, sums):
        def ahead_y(c):
            edge = jnp.where(has_after, yhalo[1, c, pl.ds(x, 1), :], 0.0)
            return jnp.where(last_row, edge, pltpu.roll(field[c, x + 1], cy - 1, 0))

        def behind_y(c):
            edge = jnp.where(has_before, yhalo[0, c, pl.ds(x, 1), :], 0.0)
            return jnp.where(first_row, edge, pltpu.roll(field[c, x + 1], 1, 0))

        neighbours = [
            (lambda c: field[c, x + 2], lambda c: field[c, x]),
            (ahead_y, behind_y),
            (lambda c: pltpu.roll(field[c, x + 1], nz - 1, 1), lambda c: pltpu.roll(field[c, x + 1], 1, 1)),
        ]
        own = [field[c, x + 1] for c in range(3)]
        own_visc = field[6, x + 1]
        change = [jnp.zeros_like(own_visc) for c in range(3)]
        for d, (forward, backward) in enumerate(neighbours):
            factor = 0.5 * own[d]
            face_ahead = 0.5 * (own_visc + forward(6))
            face_behind = 0.5 * (own_visc + backward(6))
            for c in range(3):
                change[c] += factor * (forward(3 + c) - backward(3 + c))
                change[c] += face_ahead * (forward(c) - own[c])
                change[c] += face_behind * (backward(c) - own[c])
        result = []
        for c in range(3):
            start = pl.multiple_of(c * cx * cy + x * cy, cy)
            value = own[c] + time_step * change[c] + total[pl.ds(start, cy), :]
            out[c, x] = value
            result.append(sums[c] + jnp.sum(value, axis=0, keepdims=True))
        return tuple(result)

    sums = lax.fori_loop(0, cx, plane, tuple(jnp.zeros((1, nz), F32) for c in range(3)))
    lanes = moment.shape[1]
    levels = nz // CB
    group = jnp.where(iota((nz, lanes), 0) // CB + pencil * levels == iota((nz, lanes), 1), 1.0, 0.0)
    stacked = jnp.concatenate(list(sums) + [jnp.zeros((5, nz), F32)], axis=0)
    moment[...] = jnp.dot(stacked, group, precision=HIGH, preferred_element_type=F32)


def far_kernel(
    n_slab, n_pencil, cx, cy, sigma, moment, out, inbox, slab_moment, everywhere, asend, arecv, bsend, brecv
):
    slab, pencil = lax.axis_index("slab"), lax.axis_index("pencil")
    barrier = pltpu.get_barrier_semaphore()
    signal_peers("pencil", pencil, n_pencil, (1, n_pencil))
    signal_peers("slab", slab, n_slab, (1, n_slab))
    pl.semaphore_wait(barrier, n_slab - 1 + n_pencil - 1)

    def to_pencil(k, carry):
        remote(moment, inbox.at[k], asend, arecv, {"pencil": lax.rem(pencil + k, n_pencil)}).start()
        return carry

    lax.fori_loop(1, n_pencil, to_pencil, 0)
    inbox[0] = moment[...]
    arrived = remote(inbox.at[1:n_pencil], inbox.at[1:n_pencil], asend, arecv, {"pencil": lax.rem(pencil + 1, n_pencil)})
    arrived.wait_recv()
    slab_moment[...] = jnp.sum(inbox[...], axis=0)

    def to_slab(k, carry):
        peer = lax.rem(slab + k, n_slab)
        remote(slab_moment, everywhere.at[slab], bsend, brecv, {"slab": peer}).start()
        return carry

    lax.fori_loop(1, n_slab, to_slab, 0)
    everywhere[slab] = slab_moment[...]
    gathered = remote(
        everywhere.at[1:n_slab], everywhere.at[1:n_slab], bsend, brecv, {"slab": lax.rem(slab + 1, n_slab)}
    )
    gathered.wait_recv()
    arrived.wait_send()
    gathered.wait_send()

    lanes = moment.shape[1]
    levels = lanes // n_pencil
    shape = (n_slab, lanes)
    rel_x = ((slab - iota(shape, 0)) * cx).astype(F32)
    rel_y = ((pencil - iota(shape, 1) // levels) * cy).astype(F32)
    level = iota(shape, 1) % levels
    plane_sq = rel_x * rel_x + rel_y * rel_y + sigma * sigma
    m0, m1, m2 = (everywhere[:, c, :] for c in range(3))
    fixed = (-(rel_y * m2), rel_x * m2, rel_y * m0 - rel_x * m1)
    sums = ([], [], [])
    for target in range(levels):
        rel_z = ((target - level) * CB).astype(F32)
        inverse = lax.rsqrt(plane_sq + rel_z * rel_z)
        weight = inverse * inverse * inverse
        terms = (rel_z * m1 + fixed[0], fixed[1] - rel_z * m0, fixed[2])
        for c in range(3):
            sums[c].append(jnp.sum(weight * terms[c], axis=0, keepdims=True))
    ones = jnp.ones((8, lanes), F32)
    for c in range(3):
        rows = jnp.concatenate(sums[c], axis=0)
        out[c, 0] = lax.dot_general(
            ones, rows, (((1,), (1,)), ((), ())), precision=HIGH, preferred_element_type=F32
        )[0:1]


def per_device(n_slab, n_pencil, vorticity, velocity, viscosity, tile_weights, tile_cells, tile_dest, tile_count):
    _, cx, cy, nz = vorticity.shape
    tile_len = tile_weights.shape[2]
    levels = nz // CB
    lanes = n_pencil * levels
    hbm = pl.BlockSpec(memory_space=pl.ANY)
    vmem = pl.BlockSpec(memory_space=pltpu.VMEM)
    smem = pl.BlockSpec(memory_space=pltpu.SMEM)
    dma = pltpu.SemaphoreType.DMA
    tiles, xhalo, yhalo = pl.pallas_call(
        functools.partial(exchange_kernel, n_slab, n_pencil),
        out_shape=(
            jax.ShapeDtypeStruct((n_slab, 8, tile_len), F32),
            jax.ShapeDtypeStruct((2, FIELDS, cy, nz), F32),
            jax.ShapeDtypeStruct((2, FIELDS, cx, nz), F32),
        ),
        in_specs=[hbm, hbm, hbm, vmem, vmem, vmem, smem],
        out_specs=(vmem, vmem, vmem),
        scratch_shapes=[
            pltpu.VMEM((FIELDS, cx, cy, nz), F32),
            pltpu.VMEM((n_slab, 8, tile_len), F32),
            pltpu.VMEM((2, FIELDS, cx, nz), F32),
            dma((3,)), dma((2,)), dma((2,)), dma((2,)), dma((2,)), dma, dma,
        ],
        compiler_params=pltpu.CompilerParams(collective_id=0, has_side_effects=True, vmem_limit_bytes=24 << 20),
        name="exchange",
    )(vorticity, velocity, viscosity, jnp.transpose(tile_weights, (1, 0, 2)), tile_cells, tile_dest.reshape(1, -1), tile_count)
    vorticity_out, moment = pl.pallas_call(
        functools.partial(block_kernel, n_slab, n_pencil),
        out_shape=(
            jax.ShapeDtypeStruct(vorticity.shape, F32),
            jax.ShapeDtypeStruct((8, lanes), F32),
        ),
        in_specs=[hbm, hbm, hbm, vmem, vmem, vmem],
        out_specs=(vmem, vmem),
        scratch_shapes=[
            pltpu.VMEM((FIELDS, cx + 2, cy, nz), F32),
            pltpu.VMEM((3 * cx * cy, 4 * tile_len), BF16),
            pltpu.VMEM((nz, 4 * tile_len), BF16),
            pltpu.VMEM((3 * cx * cy, nz), F32),
            dma((3,)),
        ],
        compiler_params=pltpu.CompilerParams(vmem_limit_bytes=40 << 20),
        name="block",
    )(vorticity, velocity, viscosity, xhalo, yhalo, tiles)
    far_velocity = pl.pallas_call(
        functools.partial(far_kernel, n_slab, n_pencil, cx, cy, float(cx * n_slab // 4)),
        out_shape=jax.ShapeDtypeStruct((3, 1, 1, levels), F32),
        in_specs=[vmem],
        out_specs=vmem,
        scratch_shapes=[
            pltpu.VMEM((n_pencil, 8, lanes), F32),
            pltpu.VMEM((8, lanes), F32),
            pltpu.VMEM((n_slab, 8, lanes), F32),
            dma, dma, dma, dma,
        ],
        compiler_params=pltpu.CompilerParams(collective_id=1, has_side_effects=True, vmem_limit_bytes=24 << 20),
        name="far",
    )(moment)
    return vorticity_out, far_velocity


def solution(mesh):
    in_specs = (
        P(None, "slab", "pencil", None),
        P(None, "slab", "pencil", None),
        P("slab", "pencil", None),
        P(("slab", "pencil"), None, None),
        P(("slab", "pencil"), None),
        P(("slab", "pencil"), None),
        P(("slab", "pencil")),
    )
    out_specs = (P(None, "slab", "pencil", None), P(None, "slab", "pencil", None))
    step = functools.partial(per_device, mesh.shape["slab"], mesh.shape["pencil"])
    return jax.shard_map(step, mesh=mesh, in_specs=in_specs, out_specs=out_specs, check_vma=False)
```

```python
import functools

import jax
import jax.numpy as jnp
from jax import lax
from jax.experimental import pallas as pl
from jax.experimental.pallas import tpu as pltpu
from jax.sharding import PartitionSpec as P

CB = 16
FIELDS = 7
time_step = 0.1
VMEM_LIMIT = 60 << 20
HIGH = lax.Precision.HIGHEST
F32 = jnp.float32
BF16 = jnp.bfloat16
MESH = pl.DeviceIdType.MESH


def iota(shape, dim):
    return lax.broadcasted_iota(jnp.int32, shape, dim)


def signal_peers(axis, me, count, offsets):
    barrier = pltpu.get_barrier_semaphore()

    def one(k, carry):
        peer = lax.rem(me + k, count)
        pl.semaphore_signal(barrier, inc=1, device_id={axis: peer}, device_id_type=MESH)
        return carry

    lax.fori_loop(offsets[0], offsets[1], one, 0)


def remote(src, dst, send_sem, recv_sem, device):
    return pltpu.make_async_remote_copy(
        src_ref=src, dst_ref=dst, send_sem=send_sem, recv_sem=recv_sem, device_id=device, device_id_type=MESH
    )


def pack_tiles(weights, cells, dest, live, send, n_slab):
    tiles = cells.shape[0]
    slab = iota((n_slab, tiles), 0)
    tile = iota((n_slab, tiles), 1)
    match = jnp.where((dest[...] == slab) & (tile < live), 1.0, 0.0)
    earlier = jnp.where(iota((tiles, tiles), 0) < iota((tiles, tiles), 1), 1.0, 0.0)
    before = jnp.dot(match, earlier, preferred_element_type=F32)
    for j in range(2):
        pick = jnp.where(before == j, match, 0.0)
        for c in range(4):
            rows = weights[c] if c < 3 else (cells[...] + 1).astype(F32)
            send[:, 4 * j + c, :] = jnp.dot(pick, rows, precision=HIGH, preferred_element_type=F32)


def deposit(tiles, lhs, rhs, total, first, last):
    rows, nz = total.shape[0] // 3, total.shape[1]
    width = 2 * tiles.shape[2]
    group = lhs.shape[1] // (2 * width)
    shift = nz.bit_length() - 1
    number = iota((rows, width), 0).astype(F32).astype(BF16)
    one, zero = jnp.ones((), BF16), jnp.zeros((), BF16)

    def add(i, carry):
        for g in range(group):
            tile = tiles[i * group + g]
            entry = [jnp.concatenate([tile[c : c + 1], tile[4 + c : 5 + c]], axis=1) for c in range(4)]
            cell = entry[3].astype(jnp.int32) - 1
            high = (cell >> shift).astype(F32).astype(BF16)
            low = (cell & (nz - 1)).astype(F32).astype(BF16)
            here = number == high
            at = 2 * g * width
            for c in range(3):
                first_piece = entry[c].astype(BF16)
                second_piece = (entry[c] - first_piece.astype(F32)).astype(BF16)
                lhs[c * rows : (c + 1) * rows, at : at + width] = jnp.where(here, first_piece, zero)
                lhs[c * rows : (c + 1) * rows, at + width : at + 2 * width] = jnp.where(here, second_piece, zero)
            onehot = jnp.where(number == low, one, zero)
            rhs[:, at : at + width] = onehot
            rhs[:, at + width : at + 2 * width] = onehot
        total[...] += lax.dot_general(lhs[...], rhs[...], (((1,), (1,)), ((), ())), preferred_element_type=F32)
        return carry

    lax.fori_loop(first, last, add, 0)


def tile_moments(tiles, nz, base, lanes):
    levels = nz // CB
    sums = [[None] * levels for c in range(3)]
    for j in range(2):
        code = tiles[:, 4 * j + 3, :].astype(jnp.int32) - 1
        level = (code & (nz - 1)) // CB
        for l in range(levels):
            here = level == l
            for c in range(3):
                part = jnp.where(here, tiles[:, 4 * j + c, :], 0.0)
                part = jnp.sum(part.reshape(part.shape[0] // 8, 8, part.shape[1]), axis=0)
                sums[c][l] = part if j == 0 else sums[c][l] + part
    place = jnp.where(iota((8 * levels, lanes), 0) // 8 + base == iota((8 * levels, lanes), 1), 1.0, 0.0)
    ones = jnp.ones((8, tiles.shape[2]), F32)
    rows = []
    for c in range(3):
        stacked = jnp.concatenate(sums[c], axis=0)
        line = lax.dot_general(ones, stacked, (((1,), (1,)), ((), ())), precision=HIGH, preferred_element_type=F32)
        rows.append(jnp.dot(line, place, precision=HIGH, preferred_element_type=F32)[0:1])
    return jnp.concatenate(rows + [jnp.zeros((5, lanes), F32)], axis=0)


def step_kernel(
    n_slab, n_pencil, sigma, vort, velo, visc, weights, cells, dest, count,
    out, far,
    field, wtile, ctile, send, tiles, yface, yhalo, lhs, rhs, total, moment, inbox, slab_moment, everywhere,
    load_sem, xsend, xrecv, ysend, yrecv, tsend, trecv, asend, arecv, bsend, brecv,
):
    slab, pencil = lax.axis_index("slab"), lax.axis_index("pencil")
    cx, cy, nz = out.shape[1], out.shape[2], out.shape[3]
    lanes = moment.shape[1]
    levels = nz // CB
    tile_loads = [
        pltpu.make_async_copy(weights, wtile, load_sem.at[3]),
        pltpu.make_async_copy(cells, ctile, load_sem.at[4]),
    ]
    loads = [
        pltpu.make_async_copy(vort, field.at[0:3, 1 : cx + 1], load_sem.at[0]),
        pltpu.make_async_copy(velo, field.at[3:6, 1 : cx + 1], load_sem.at[1]),
        pltpu.make_async_copy(visc, field.at[6, 1 : cx + 1], load_sem.at[2]),
    ]
    for load in tile_loads + loads:
        load.start()
    barrier = pltpu.get_barrier_semaphore()
    signal_peers("slab", slab, n_slab, (1, n_slab))
    signal_peers("pencil", pencil, n_pencil, (1, n_pencil))
    for load in tile_loads:
        load.wait()
    pack_tiles(wtile, ctile, dest, count[0], send, n_slab)
    total[...] = jnp.zeros_like(total)
    for load in loads:
        load.wait()
    for c in range(FIELDS):
        yface[0, c] = field[c, 1 : cx + 1, 0, :]
        yface[1, c] = field[c, 1 : cx + 1, cy - 1, :]
    pl.semaphore_wait(barrier, n_slab - 1 + n_pencil - 1)

    s_up, s_down = lax.rem(slab + 1, n_slab), lax.rem(slab + n_slab - 1, n_slab)
    p_up, p_down = lax.rem(pencil + 1, n_pencil), lax.rem(pencil + n_pencil - 1, n_pencil)
    yhalos = [
        remote(yface.at[0], yhalo.at[1], ysend.at[0], yrecv.at[1], {"pencil": p_down}),
        remote(yface.at[1], yhalo.at[0], ysend.at[1], yrecv.at[0], {"pencil": p_up}),
    ]
    xhalos = [
        remote(field.at[:, 1], field.at[:, cx + 1], xsend.at[0], xrecv.at[1], {"slab": s_down}),
        remote(field.at[:, cx], field.at[:, 0], xsend.at[1], xrecv.at[0], {"slab": s_up}),
    ]
    for halo in yhalos + xhalos:
        halo.start()

    def deliver(k, carry):
        peer = lax.rem(slab + k, n_slab)
        remote(send.at[peer], tiles.at[k], tsend, trecv, {"slab": peer}).start()
        return carry

    lax.fori_loop(1, n_slab, deliver, 0)
    tiles[0] = send[slab]
    delivered = remote(send.at[1:n_slab], tiles.at[1:n_slab], tsend, trecv, {"slab": s_up})
    for halo in yhalos:
        halo.wait()

    row = iota((cy, nz), 0)
    first_row, last_row = row == 0, row == cy - 1
    has_before, has_after = pencil > 0, pencil < n_pencil - 1

    def plane(x, sums):
        def ahead_y(c):
            edge = jnp.where(has_after, yhalo[1, c, pl.ds(x, 1), :], 0.0)
            return jnp.where(last_row, edge, pltpu.roll(field[c, x + 1], cy - 1, 0))

        def behind_y(c):
            edge = jnp.where(has_before, yhalo[0, c, pl.ds(x, 1), :], 0.0)
            return jnp.where(first_row, edge, pltpu.roll(field[c, x + 1], 1, 0))

        neighbours = [
            (lambda c: field[c, x + 2], lambda c: field[c, x]),
            (ahead_y, behind_y),
            (lambda c: pltpu.roll(field[c, x + 1], nz - 1, 1), lambda c: pltpu.roll(field[c, x + 1], 1, 1)),
        ]
        own = [field[c, x + 1] for c in range(3)]
        own_visc = field[6, x + 1]
        change = [jnp.zeros_like(own_visc) for c in range(3)]
        for d, (forward, backward) in enumerate(neighbours):
            factor = 0.5 * own[d]
            face_ahead = 0.5 * (own_visc + forward(6))
            face_behind = 0.5 * (own_visc + backward(6))
            for c in range(3):
                change[c] += factor * (forward(3 + c) - backward(3 + c))
                change[c] += face_ahead * (forward(c) - own[c])
                change[c] += face_behind * (backward(c) - own[c])
        result = []
        for c in range(3):
            value = own[c] + time_step * change[c]
            out[c, x] = value
            result.append(sums[c] + jnp.sum(value, axis=0, keepdims=True))
        return tuple(result)

    sums = lax.fori_loop(1, cx - 1, plane, tuple(jnp.zeros((1, nz), F32) for c in range(3)))
    for halo in xhalos:
        halo.wait()
    field[:, 0] = jnp.where(slab > 0, field[:, 0], 0.0)
    field[:, cx + 1] = jnp.where(slab < n_slab - 1, field[:, cx + 1], 0.0)
    sums = lax.fori_loop(0, 2, lambda i, sums: plane(i * (cx - 1), sums), sums)
    delivered.wait_recv()
    group = jnp.where(iota((nz, lanes), 0) // CB + pencil * levels == iota((nz, lanes), 1), 1.0, 0.0)
    stacked = jnp.concatenate(list(sums) + [jnp.zeros((5, nz), F32)], axis=0)
    moment[...] = jnp.dot(stacked, group, precision=HIGH, preferred_element_type=F32) + tile_moments(
        tiles, nz, pencil * levels, lanes
    )

    def to_pencil(k, carry):
        remote(moment, inbox.at[k], asend, arecv, {"pencil": lax.rem(pencil + k, n_pencil)}).start()
        return carry

    lax.fori_loop(1, n_pencil, to_pencil, 0)
    inbox[0] = moment[...]
    arrived = remote(inbox.at[1:n_pencil], inbox.at[1:n_pencil], asend, arecv, {"pencil": p_up})
    groups = tiles.shape[0] * 4 * tiles.shape[2] // lhs.shape[1]
    deposit(tiles, lhs, rhs, total, 0, groups * 3 // 8)
    arrived.wait_recv()
    slab_moment[...] = jnp.sum(inbox[...], axis=0)

    def to_slab(k, carry):
        peer = lax.rem(slab + k, n_slab)
        remote(slab_moment, everywhere.at[slab], bsend, brecv, {"slab": peer}).start()
        return carry

    lax.fori_loop(1, n_slab, to_slab, 0)
    everywhere[slab] = slab_moment[...]
    gathered = remote(everywhere.at[1:n_slab], everywhere.at[1:n_slab], bsend, brecv, {"slab": s_up})
    deposit(tiles, lhs, rhs, total, groups * 3 // 8, groups)
    for c in range(3):
        out[c] += total[c * cx * cy : (c + 1) * cx * cy].reshape(cx, cy, nz)
    gathered.wait_recv()
    delivered.wait_send()
    arrived.wait_send()
    gathered.wait_send()

    shape = (n_slab, lanes)
    rel_x = ((slab - iota(shape, 0)) * cx).astype(F32)
    rel_y = ((pencil - iota(shape, 1) // levels) * cy).astype(F32)
    level = iota(shape, 1) % levels
    plane_sq = rel_x * rel_x + rel_y * rel_y + sigma * sigma
    m0, m1, m2 = (everywhere[:, c, :] for c in range(3))
    fixed = (-(rel_y * m2), rel_x * m2, rel_y * m0 - rel_x * m1)
    far_sums = ([], [], [])
    for target in range(levels):
        rel_z = ((target - level) * CB).astype(F32)
        inverse = lax.rsqrt(plane_sq + rel_z * rel_z)
        weight = inverse * inverse * inverse
        terms = (rel_z * m1 + fixed[0], fixed[1] - rel_z * m0, fixed[2])
        for c in range(3):
            far_sums[c].append(jnp.sum(weight * terms[c], axis=0, keepdims=True))
    ones = jnp.ones((8, lanes), F32)
    for c in range(3):
        rows = jnp.concatenate(far_sums[c], axis=0)
        far[c, 0] = lax.dot_general(ones, rows, (((1,), (1,)), ((), ())), precision=HIGH, preferred_element_type=F32)[0:1]


GROUP = 4


def per_device(n_slab, n_pencil, vorticity, velocity, viscosity, tile_weights, tile_cells, tile_dest, tile_count):
    _, cx, cy, nz = vorticity.shape
    n_tiles, tile_len = tile_cells.shape
    levels = nz // CB
    lanes = n_pencil * levels
    hbm = pl.BlockSpec(memory_space=pltpu.HBM)
    vmem = pl.BlockSpec(memory_space=pltpu.VMEM)
    smem = pl.BlockSpec(memory_space=pltpu.SMEM)
    dma = pltpu.SemaphoreType.DMA
    return pl.pallas_call(
        functools.partial(step_kernel, n_slab, n_pencil, float(cx * n_slab // 4)),
        out_shape=(jax.ShapeDtypeStruct(vorticity.shape, F32), jax.ShapeDtypeStruct((3, 1, 1, levels), F32)),
        in_specs=[hbm, hbm, hbm, hbm, hbm, vmem, smem],
        out_specs=(vmem, vmem),
        scratch_shapes=[
            pltpu.VMEM((FIELDS, cx + 2, cy, nz), F32),
            pltpu.VMEM((3, n_tiles, tile_len), F32),
            pltpu.VMEM((n_tiles, tile_len), jnp.int32),
            pltpu.VMEM((n_slab, 8, tile_len), F32),
            pltpu.VMEM((n_slab, 8, tile_len), F32),
            pltpu.VMEM((2, FIELDS, cx, nz), F32),
            pltpu.VMEM((2, FIELDS, cx, nz), F32),
            pltpu.VMEM((3 * cx * cy, GROUP * 4 * tile_len), BF16),
            pltpu.VMEM((nz, GROUP * 4 * tile_len), BF16),
            pltpu.VMEM((3 * cx * cy, nz), F32),
            pltpu.VMEM((8, lanes), F32),
            pltpu.VMEM((n_pencil, 8, lanes), F32),
            pltpu.VMEM((8, lanes), F32),
            pltpu.VMEM((n_slab, 8, lanes), F32),
            dma((5,)), dma((2,)), dma((2,)), dma((2,)), dma((2,)), dma, dma, dma, dma, dma, dma,
        ],
        compiler_params=pltpu.CompilerParams(collective_id=0, has_side_effects=True, vmem_limit_bytes=VMEM_LIMIT),
        name="step",
    )(
        vorticity, velocity, viscosity, jnp.transpose(tile_weights, (1, 0, 2)), tile_cells,
        tile_dest.reshape(1, -1), tile_count,
    )


def solution(mesh):
    in_specs = (
        P(None, "slab", "pencil", None),
        P(None, "slab", "pencil", None),
        P("slab", "pencil", None),
        P(("slab", "pencil"), None, None),
        P(("slab", "pencil"), None),
        P(("slab", "pencil"), None),
        P(("slab", "pencil")),
    )
    out_specs = (P(None, "slab", "pencil", None), P(None, "slab", "pencil", None))
    step = functools.partial(per_device, mesh.shape["slab"], mesh.shape["pencil"])
    return jax.shard_map(step, mesh=mesh, in_specs=in_specs, out_specs=out_specs, check_vma=False)
```

```python
import functools

import jax
import jax.numpy as jnp
from jax import lax
from jax.experimental import pallas as pl
from jax.experimental.pallas import tpu as pltpu
from jax.sharding import PartitionSpec as P

CB = 16
FIELDS = 7
time_step = 0.1
VMEM_LIMIT = 60 << 20
HIGH = lax.Precision.HIGHEST
F32 = jnp.float32
BF16 = jnp.bfloat16
MESH = pl.DeviceIdType.MESH


def iota(shape, dim):
    return lax.broadcasted_iota(jnp.int32, shape, dim)


def offset(i):
    return (2 * (i % 2) - 1) * ((i + 1) // 2)


def far_first(first, last, one):
    def body(j, carry):
        one(last - j)
        return carry

    lax.fori_loop(0, last - first + 1, body, 0)


def remote(src, dst, send_sem, recv_sem, device):
    return pltpu.make_async_remote_copy(
        src_ref=src, dst_ref=dst, send_sem=send_sem, recv_sem=recv_sem, device_id=device, device_id_type=MESH
    )


def pack_tiles(weights, cells, dest, live, send, sums, nz):
    n_slab = send.shape[0]
    tiles, lanes = cells.shape
    slab = iota((n_slab, tiles), 0)
    tile = iota((n_slab, tiles), 1)
    match = jnp.where((dest[...] == slab) & (tile < live), 1.0, 0.0)
    earlier = jnp.where(iota((tiles, tiles), 0) < iota((tiles, tiles), 1), 1.0, 0.0)
    before = jnp.dot(match, earlier, preferred_element_type=F32)
    for j in range(2):
        pick = jnp.where(before == j, match, 0.0)
        for c in range(4):
            rows = weights[c] if c < 3 else (cells[...] + 1).astype(F32)
            send[:, 4 * j + c, :] = jnp.dot(pick, rows, precision=HIGH, preferred_element_type=F32)
    levels = nz // CB
    level = (cells[...] & (nz - 1)) // CB
    lane = iota((tiles, lanes), 1)
    by_level = jnp.zeros((tiles, lanes), F32)
    for l in range(levels):
        here = level == l
        for c in range(3):
            total = jnp.sum(jnp.where(here, weights[c], 0.0), axis=1, keepdims=True)
            by_level = jnp.where(lane == c * levels + l, total, by_level)
    sums[:, 0, :] = jnp.dot(match, by_level, precision=HIGH, preferred_element_type=F32)


def deposit(tiles, lhs, rhs, total, first, last):
    rows, nz = total.shape[0] // 3, total.shape[1]
    width = 2 * tiles.shape[2]
    group = lhs.shape[1] // (2 * width)
    shift = nz.bit_length() - 1
    number = iota((rows, width), 0).astype(F32).astype(BF16)
    one, zero = jnp.ones((), BF16), jnp.zeros((), BF16)

    def add(i, carry):
        for g in range(group):
            tile = tiles[i * group + g]
            entry = [jnp.concatenate([tile[c : c + 1], tile[4 + c : 5 + c]], axis=1) for c in range(4)]
            cell = entry[3].astype(jnp.int32) - 1
            high = (cell >> shift).astype(F32).astype(BF16)
            low = (cell & (nz - 1)).astype(F32).astype(BF16)
            here = number == high
            at = 2 * g * width
            for c in range(3):
                first_piece = entry[c].astype(BF16)
                second_piece = (entry[c] - first_piece.astype(F32)).astype(BF16)
                lhs[c * rows : (c + 1) * rows, at : at + width] = jnp.where(here, first_piece, zero)
                lhs[c * rows : (c + 1) * rows, at + width : at + 2 * width] = jnp.where(here, second_piece, zero)
            onehot = jnp.where(number == low, one, zero)
            rhs[:, at : at + width] = onehot
            rhs[:, at + width : at + 2 * width] = onehot
        total[...] += lax.dot_general(lhs[...], rhs[...], (((1,), (1,)), ((), ())), preferred_element_type=F32)
        return carry

    lax.fori_loop(first, last, add, 0)


def step_kernel(
    n_slab, n_pencil, sigma, vort, velo, visc, weights, cells, dest, count,
    out_hbm, far,
    field, wtile, ctile, send, tiles, sums_send, sums_in, yface, yhalo, lhs, rhs, total, out, moment, inbox, slab_moment,
    everywhere, load_sem, xsend, xrecv, ysend, yrecv, tsend, trecv, msend, mrecv, asend, arecv, bsend, brecv, ready, out_sem,
):
    slab, pencil = lax.axis_index("slab"), lax.axis_index("pencil")
    cx, cy, nz = out.shape[1], out.shape[2], out.shape[3]
    lanes = moment.shape[1]
    levels = nz // CB
    waves = [min(2 * NEAR, n_slab - 1)]
    while waves[-1] < n_slab - 1:
        waves.append(min(2 * waves[-1], n_slab - 1))

    def slab_peer(i):
        return {"slab": lax.rem(slab + offset(i) + n_slab, n_slab)}

    def pencil_peer(i):
        return {"pencil": lax.rem(pencil + offset(i) + n_pencil, n_pencil)}

    loads = [
        pltpu.make_async_copy(vort, field.at[0:3, 1 : cx + 1], load_sem.at[0]),
        pltpu.make_async_copy(velo, field.at[3:6, 1 : cx + 1], load_sem.at[1]),
        pltpu.make_async_copy(visc, field.at[6, 1 : cx + 1], load_sem.at[2]),
    ]
    tile_loads = [
        pltpu.make_async_copy(weights, wtile, load_sem.at[3]),
        pltpu.make_async_copy(cells, ctile, load_sem.at[4]),
    ]
    for load in loads + tile_loads:
        load.start()
    barrier = pltpu.get_barrier_semaphore()

    def greet(where):
        pl.semaphore_signal(barrier, inc=1, device_id=where, device_id_type=MESH)

    far_first(1, waves[0], lambda i: greet(slab_peer(i)))
    far_first(1, n_pencil - 1, lambda i: greet(pencil_peer(i)))
    for load in loads:
        load.wait()
    for c in range(FIELDS):
        yface[0, c] = field[c, 1 : cx + 1, 0, :]
        yface[1, c] = field[c, 1 : cx + 1, cy - 1, :]
    pl.semaphore_wait(barrier, waves[0] + n_pencil - 1)

    s_up, s_down = slab_peer(1), slab_peer(2)
    p_up, p_down = pencil_peer(1), pencil_peer(2)
    yhalos = [
        remote(yface.at[0], yhalo.at[1], ysend.at[0], yrecv.at[1], p_down),
        remote(yface.at[1], yhalo.at[0], ysend.at[1], yrecv.at[0], p_up),
    ]
    xhalos = [
        remote(field.at[:, 1], field.at[:, cx + 1], xsend.at[0], xrecv.at[1], s_down),
        remote(field.at[:, cx], field.at[:, 0], xsend.at[1], xrecv.at[0], s_up),
    ]
    for halo in yhalos + xhalos:
        halo.start()

    def announce(step):
        for i in (waves[step] - 1, waves[step]):
            pl.semaphore_signal(ready.at[step], inc=1, device_id=slab_peer(i), device_id_type=MESH)

    def destination(i):
        return lax.rem(slab + offset(i) + n_slab, n_slab)

    def send_sums(i):
        remote(
            sums_send.at[destination(i), 0:1], sums_in.at[i, 0:1], msend, mrecv, slab_peer(i)
        ).start()

    def send_tiles(wave):
        first = 1 if wave == 0 else waves[wave - 1] + 1

        def one(i):
            remote(send.at[destination(i)], tiles.at[i], tsend.at[wave], trecv.at[wave], slab_peer(i)).start()

        far_first(first, waves[wave], one)

    def tiles_of(wave):
        first = 1 if wave == 0 else waves[wave - 1] + 1
        part = slice(first, waves[wave] + 1)
        return remote(send.at[part], tiles.at[part], tsend.at[wave], trecv.at[wave], s_up)

    if len(waves) > 1:
        announce(0)
    for load in tile_loads:
        load.wait()
    pack_tiles(wtile, ctile, dest, count[0], send, sums_send, nz)
    tiles[0] = send[slab]
    sums_in[0, 0:1] = sums_send[slab, 0:1]
    total[...] = jnp.zeros_like(total)
    if len(waves) > 1:
        pl.semaphore_wait(ready.at[0], 2)
    for step in range(1, len(waves) - 1):
        announce(step)
    for halo in yhalos:
        halo.wait()

    row = iota((cy, nz), 0)
    first_row, last_row = row == 0, row == cy - 1
    has_before, has_after = pencil > 0, pencil < n_pencil - 1

    def plane(x, sums):
        def ahead_y(c):
            edge = jnp.where(has_after, yhalo[1, c, pl.ds(x, 1), :], 0.0)
            return jnp.where(last_row, edge, pltpu.roll(field[c, x + 1], cy - 1, 0))

        def behind_y(c):
            edge = jnp.where(has_before, yhalo[0, c, pl.ds(x, 1), :], 0.0)
            return jnp.where(first_row, edge, pltpu.roll(field[c, x + 1], 1, 0))

        neighbours = [
            (lambda c: field[c, x + 2], lambda c: field[c, x]),
            (ahead_y, behind_y),
            (lambda c: pltpu.roll(field[c, x + 1], nz - 1, 1), lambda c: pltpu.roll(field[c, x + 1], 1, 1)),
        ]
        own = [field[c, x + 1] for c in range(3)]
        own_visc = field[6, x + 1]
        change = [jnp.zeros_like(own_visc) for c in range(3)]
        for d, (forward, backward) in enumerate(neighbours):
            factor = 0.5 * own[d]
            face_ahead = 0.5 * (own_visc + forward(6))
            face_behind = 0.5 * (own_visc + backward(6))
            for c in range(3):
                change[c] += factor * (forward(3 + c) - backward(3 + c))
                change[c] += face_ahead * (forward(c) - own[c])
                change[c] += face_behind * (backward(c) - own[c])
        result = []
        for c in range(3):
            value = own[c] + time_step * change[c]
            out[c, x] = value
            result.append(sums[c] + jnp.sum(value, axis=0, keepdims=True))
        return tuple(result)

    sums = lax.fori_loop(1, cx - 1, plane, tuple(jnp.zeros((1, nz), F32) for c in range(3)))
    for step in range(1, len(waves) - 1):
        pl.semaphore_wait(ready.at[step], 2)
    far_first(1, n_slab - 1, send_sums)
    for wave in range(len(waves)):
        send_tiles(wave)
    for halo in xhalos:
        halo.wait()
    field[:, 0] = jnp.where(slab > 0, field[:, 0], 0.0)
    field[:, cx + 1] = jnp.where(slab < n_slab - 1, field[:, cx + 1], 0.0)
    sums = lax.fori_loop(0, 2, lambda i, sums: plane(i * (cx - 1), sums), sums)
    all_sums = remote(sums_send.at[1:n_slab, 0:1], sums_in.at[1:n_slab, 0:1], msend, mrecv, s_up)
    all_sums.wait_recv()
    line = jnp.sum(sums_in[:, 0, :], axis=0, keepdims=True)
    width = sums_in.shape[2]
    row, column = iota((8, width), 0), iota((8, width), 1)
    tile_rows = jnp.where((column // levels == row) & (row < 3), line, 0.0)
    place = jnp.where(iota((width, lanes), 0) % levels + pencil * levels == iota((width, lanes), 1), 1.0, 0.0)
    group = jnp.where(iota((nz, lanes), 0) // CB + pencil * levels == iota((nz, lanes), 1), 1.0, 0.0)
    stacked = jnp.concatenate(list(sums) + [jnp.zeros((5, nz), F32)], axis=0)
    moment[...] = jnp.dot(
        jnp.concatenate([stacked, tile_rows], axis=1), jnp.concatenate([group, place], axis=0),
        precision=HIGH, preferred_element_type=F32,
    )

    far_first(1, n_pencil - 1, lambda i: remote(moment, inbox.at[i], asend, arecv, pencil_peer(i)).start())
    inbox[0] = moment[...]
    arrived = remote(inbox.at[1:n_pencil], inbox.at[1:n_pencil], asend, arecv, p_up)
    groups = tiles.shape[0] * 4 * tiles.shape[2] // lhs.shape[1]
    early = max(1, len(waves) - 1)
    for wave in range(early):
        tiles_of(wave).wait_recv()
    deposit(tiles, lhs, rhs, total, 0, groups // 4)
    arrived.wait_recv()
    slab_moment[...] = jnp.sum(inbox[...], axis=0)
    far_first(1, n_slab - 1, lambda i: remote(slab_moment, everywhere.at[slab], bsend, brecv, slab_peer(i)).start())
    everywhere[slab] = slab_moment[...]
    gathered = remote(everywhere.at[1:n_slab], everywhere.at[1:n_slab], bsend, brecv, s_up)
    deposit(tiles, lhs, rhs, total, groups // 4, groups // 2)
    for wave in range(early, len(waves)):
        tiles_of(wave).wait_recv()
    deposit(tiles, lhs, rhs, total, groups // 2, groups)
    for c in range(3):
        out[c] += total[c * cx * cy : (c + 1) * cx * cy].reshape(cx, cy, nz)
    stores = [pltpu.make_async_copy(out.at[c], out_hbm.at[c], out_sem.at[c]) for c in range(3)]
    for store in stores:
        store.start()
    gathered.wait_recv()

    shape = (n_slab, lanes)
    rel_x = ((slab - iota(shape, 0)) * cx).astype(F32)
    rel_y = ((pencil - iota(shape, 1) // levels) * cy).astype(F32)
    level = iota(shape, 1) % levels
    plane_sq = rel_x * rel_x + rel_y * rel_y + sigma * sigma
    m0, m1, m2 = (everywhere[:, c, :] for c in range(3))
    fixed = (-(rel_y * m2), rel_x * m2, rel_y * m0 - rel_x * m1)
    far_sums = ([], [], [])
    for target in range(levels):
        rel_z = ((target - level) * CB).astype(F32)
        inverse = lax.rsqrt(plane_sq + rel_z * rel_z)
        weight = inverse * inverse * inverse
        terms = (rel_z * m1 + fixed[0], fixed[1] - rel_z * m0, fixed[2])
        for c in range(3):
            far_sums[c].append(jnp.sum(weight * terms[c], axis=0, keepdims=True))
    ones = jnp.ones((8, lanes), F32)
    for c in range(3):
        rows = jnp.concatenate(far_sums[c], axis=0)
        far[c, 0] = lax.dot_general(ones, rows, (((1,), (1,)), ((), ())), precision=HIGH, preferred_element_type=F32)[0:1]
    all_sums.wait_send()
    for wave in range(len(waves)):
        tiles_of(wave).wait_send()
    arrived.wait_send()
    gathered.wait_send()
    for store in stores:
        store.wait()


def hand_out_kernel(field, far, field_out, far_out, sem):
    copies = [pltpu.make_async_copy(field.at[c], field_out.at[c], sem.at[c]) for c in range(3)]
    for copy in copies:
        copy.start()
    far_out[...] = far[...]
    for copy in copies:
        copy.wait()


NEAR = 4
GROUP = 4


def per_device(n_slab, n_pencil, vorticity, velocity, viscosity, tile_weights, tile_cells, tile_dest, tile_count):
    _, cx, cy, nz = vorticity.shape
    n_tiles, tile_len = tile_cells.shape
    levels = nz // CB
    lanes = n_pencil * levels
    hbm = pl.BlockSpec(memory_space=pltpu.HBM)
    vmem = pl.BlockSpec(memory_space=pltpu.VMEM)
    smem = pl.BlockSpec(memory_space=pltpu.SMEM)
    dma = pltpu.SemaphoreType.DMA
    outs = (jax.ShapeDtypeStruct(vorticity.shape, F32), jax.ShapeDtypeStruct((3, 1, 1, levels), F32))
    field, far = pl.pallas_call(
        functools.partial(step_kernel, n_slab, n_pencil, float(cx * n_slab // 4)),
        out_shape=outs,
        in_specs=[hbm, hbm, hbm, hbm, hbm, vmem, smem],
        out_specs=(hbm, vmem),
        scratch_shapes=[
            pltpu.VMEM((FIELDS, cx + 2, cy, nz), F32),
            pltpu.VMEM((3, n_tiles, tile_len), F32),
            pltpu.VMEM((n_tiles, tile_len), jnp.int32),
            pltpu.VMEM((n_slab, 8, tile_len), F32),
            pltpu.VMEM((n_slab, 8, tile_len), F32),
            pltpu.VMEM((n_slab, 8, tile_len), F32),
            pltpu.VMEM((n_slab, 8, tile_len), F32),
            pltpu.VMEM((2, FIELDS, cx, nz), F32),
            pltpu.VMEM((2, FIELDS, cx, nz), F32),
            pltpu.VMEM((3 * cx * cy, GROUP * 4 * tile_len), BF16),
            pltpu.VMEM((nz, GROUP * 4 * tile_len), BF16),
            pltpu.VMEM((3 * cx * cy, nz), F32),
            pltpu.VMEM((3, cx, cy, nz), F32),
            pltpu.VMEM((8, lanes), F32),
            pltpu.VMEM((n_pencil, 8, lanes), F32),
            pltpu.VMEM((8, lanes), F32),
            pltpu.VMEM((n_slab, 8, lanes), F32),
            dma((5,)), dma((2,)), dma((2,)), dma((2,)), dma((2,)), dma((4,)), dma((4,)), dma, dma, dma, dma, dma, dma,
            pltpu.SemaphoreType.REGULAR((4,)), dma((3,)),
        ],
        compiler_params=pltpu.CompilerParams(collective_id=0, has_side_effects=True, vmem_limit_bytes=VMEM_LIMIT),
        name="step",
    )(
        vorticity, velocity, viscosity, jnp.transpose(tile_weights, (1, 0, 2)), tile_cells,
        tile_dest.reshape(1, -1), tile_count,
    )
    return pl.pallas_call(
        hand_out_kernel,
        out_shape=outs,
        in_specs=[hbm, vmem],
        out_specs=(hbm, vmem),
        scratch_shapes=[dma((3,))],
        compiler_params=pltpu.CompilerParams(vmem_limit_bytes=VMEM_LIMIT),
        name="hand_out",
    )(field, far)


def solution(mesh):
    in_specs = (
        P(None, "slab", "pencil", None),
        P(None, "slab", "pencil", None),
        P("slab", "pencil", None),
        P(("slab", "pencil"), None, None),
        P(("slab", "pencil"), None),
        P(("slab", "pencil"), None),
        P(("slab", "pencil")),
    )
    out_specs = (P(None, "slab", "pencil", None), P(None, "slab", "pencil", None))
    step = functools.partial(per_device, mesh.shape["slab"], mesh.shape["pencil"])
    return jax.shard_map(step, mesh=mesh, in_specs=in_specs, out_specs=out_specs, check_vma=False)
```

```python
import functools

import jax
import jax.numpy as jnp
from jax import lax
from jax.experimental import pallas as pl
from jax.experimental.pallas import tpu as pltpu
from jax.sharding import PartitionSpec as P

CB = 16
FIELDS = 7
time_step = 0.1
VMEM_LIMIT = 60 << 20
HIGH = lax.Precision.HIGHEST
F32 = jnp.float32
BF16 = jnp.bfloat16
MESH = pl.DeviceIdType.MESH


def iota(shape, dim):
    return lax.broadcasted_iota(jnp.int32, shape, dim)


def offset(i):
    return (2 * (i % 2) - 1) * ((i + 1) // 2)


def far_first(first, last, one):
    def body(j, carry):
        one(last - j)
        return carry

    lax.fori_loop(0, last - first + 1, body, 0)


def remote(src, dst, send_sem, recv_sem, device):
    return pltpu.make_async_remote_copy(
        src_ref=src, dst_ref=dst, send_sem=send_sem, recv_sem=recv_sem, device_id=device, device_id_type=MESH
    )


def pack_tiles(weights, cells, dest, live, send, sums, nz):
    n_slab = send.shape[0]
    tiles, lanes = cells.shape
    slab = iota((n_slab, tiles), 0)
    tile = iota((n_slab, tiles), 1)
    match = jnp.where((dest[...] == slab) & (tile < live), 1.0, 0.0)
    earlier = jnp.where(iota((tiles, tiles), 0) < iota((tiles, tiles), 1), 1.0, 0.0)
    before = jnp.dot(match, earlier, preferred_element_type=F32)
    for j in range(2):
        pick = jnp.where(before == j, match, 0.0)
        for c in range(4):
            rows = weights[c] if c < 3 else (cells[...] + 1).astype(F32)
            send[:, 4 * j + c, :] = jnp.dot(pick, rows, precision=HIGH, preferred_element_type=F32)
    levels = nz // CB
    level = (cells[...] & (nz - 1)) // CB
    lane = iota((tiles, lanes), 1)
    by_level = jnp.zeros((tiles, lanes), F32)
    for l in range(levels):
        here = level == l
        for c in range(3):
            total = jnp.sum(jnp.where(here, weights[c], 0.0), axis=1, keepdims=True)
            by_level = jnp.where(lane == c * levels + l, total, by_level)
    row = iota((NEAR * 8, tiles), 0)
    member = jnp.where(row % 8 < n_slab // NEAR, row % 8 * NEAR + row // 8, -1)
    match = jnp.where((dest[...] == member) & (iota((NEAR * 8, tiles), 1) < live), 1.0, 0.0)
    added = jnp.dot(match, by_level, precision=HIGH, preferred_element_type=F32)
    sums[...] = added.reshape(NEAR, 8, lanes)


def deposit(tiles, lhs, rhs, total, first, last):
    rows, nz = total.shape[0] // 3, total.shape[1]
    width = 2 * tiles.shape[2]
    group = lhs.shape[1] // (2 * width)
    shift = nz.bit_length() - 1
    number = iota((rows, width), 0).astype(F32).astype(BF16)
    one, zero = jnp.ones((), BF16), jnp.zeros((), BF16)

    def add(i, carry):
        for g in range(group):
            tile = tiles[i * group + g]
            entry = [jnp.concatenate([tile[c : c + 1], tile[4 + c : 5 + c]], axis=1) for c in range(4)]
            cell = entry[3].astype(jnp.int32) - 1
            high = (cell >> shift).astype(F32).astype(BF16)
            low = (cell & (nz - 1)).astype(F32).astype(BF16)
            here = number == high
            at = 2 * g * width
            for c in range(3):
                first_piece = entry[c].astype(BF16)
                second_piece = (entry[c] - first_piece.astype(F32)).astype(BF16)
                lhs[c * rows : (c + 1) * rows, at : at + width] = jnp.where(here, first_piece, zero)
                lhs[c * rows : (c + 1) * rows, at + width : at + 2 * width] = jnp.where(here, second_piece, zero)
            onehot = jnp.where(number == low, one, zero)
            rhs[:, at : at + width] = onehot
            rhs[:, at + width : at + 2 * width] = onehot
        total[...] += lax.dot_general(lhs[...], rhs[...], (((1,), (1,)), ((), ())), preferred_element_type=F32)
        return carry

    lax.fori_loop(first, last, add, 0)


def step_kernel(
    n_slab, n_pencil, sigma, vort, velo, visc, weights, cells, dest, count,
    out_hbm, far,
    field, wtile, ctile, send, tiles, sums_send, sums_in, yface, yhalo, lhs, rhs, total, out, message, everywhere, kern,
    partial, inbox, load_sem, xsend, xrecv, ysend, yrecv, tsend, trecv, msend, mrecv, asend, arecv, bsend, brecv, ready, out_sem,
):
    slab, pencil = lax.axis_index("slab"), lax.axis_index("pencil")
    cx, cy, nz = out.shape[1], out.shape[2], out.shape[3]
    lanes = partial.shape[1]
    levels = nz // CB
    waves = [min(2 * NEAR, n_slab - 1)]
    while waves[-1] < n_slab - 1:
        waves.append(min(2 * waves[-1], n_slab - 1))

    def slab_peer(i):
        return {"slab": lax.rem(slab + offset(i) + n_slab, n_slab)}

    def pencil_peer(i):
        return {"pencil": lax.rem(pencil + offset(i) + n_pencil, n_pencil)}

    loads = [
        pltpu.make_async_copy(vort, field.at[0:3, 1 : cx + 1], load_sem.at[0]),
        pltpu.make_async_copy(velo, field.at[3:6, 1 : cx + 1], load_sem.at[1]),
        pltpu.make_async_copy(visc, field.at[6, 1 : cx + 1], load_sem.at[2]),
    ]
    tile_loads = [
        pltpu.make_async_copy(weights, wtile, load_sem.at[3]),
        pltpu.make_async_copy(cells, ctile, load_sem.at[4]),
    ]
    for load in loads + tile_loads:
        load.start()
    barrier = pltpu.get_barrier_semaphore()

    def greet(where):
        pl.semaphore_signal(barrier, inc=1, device_id=where, device_id_type=MESH)

    far_first(1, waves[0], lambda i: greet(slab_peer(i)))
    far_first(1, n_pencil - 1, lambda i: greet(pencil_peer(i)))
    for load in loads:
        load.wait()
    for c in range(FIELDS):
        yface[0, c] = field[c, 1 : cx + 1, 0, :]
        yface[1, c] = field[c, 1 : cx + 1, cy - 1, :]
    pl.semaphore_wait(barrier, waves[0] + n_pencil - 1)

    s_up, s_down = slab_peer(1), slab_peer(2)
    p_up, p_down = pencil_peer(1), pencil_peer(2)
    yhalos = [
        remote(yface.at[0], yhalo.at[1], ysend.at[0], yrecv.at[1], p_down),
        remote(yface.at[1], yhalo.at[0], ysend.at[1], yrecv.at[0], p_up),
    ]
    xhalos = [
        remote(field.at[:, 1], field.at[:, cx + 1], xsend.at[0], xrecv.at[1], s_down),
        remote(field.at[:, cx], field.at[:, 0], xsend.at[1], xrecv.at[0], s_up),
    ]
    for halo in yhalos + xhalos:
        halo.start()

    def announce(step):
        for i in (waves[step] - 1, waves[step]):
            pl.semaphore_signal(ready.at[step], inc=1, device_id=slab_peer(i), device_id_type=MESH)

    def destination(i):
        return lax.rem(slab + offset(i) + n_slab, n_slab)

    def send_tiles(wave):
        first = 1 if wave == 0 else waves[wave - 1] + 1

        def one(i):
            remote(send.at[destination(i)], tiles.at[i], tsend.at[wave], trecv.at[wave], slab_peer(i)).start()

        far_first(first, waves[wave], one)

    def tiles_of(wave):
        first = 1 if wave == 0 else waves[wave - 1] + 1
        part = slice(first, waves[wave] + 1)
        return remote(send.at[part], tiles.at[part], tsend.at[wave], trecv.at[wave], s_up)

    if len(waves) > 1:
        announce(0)
    for load in tile_loads:
        load.wait()
    pack_tiles(wtile, ctile, dest, count[0], send, sums_send, nz)
    mine = lax.rem(slab, NEAR)

    def to_member(j):
        other = lax.rem(mine + j, NEAR)
        return remote(sums_send.at[other], sums_in.at[j], msend, mrecv, {"slab": slab - mine + other})

    for j in range(1, NEAR):
        to_member(j).start()
    send_tiles(0)
    tiles[0] = send[slab]
    sums_in[0] = sums_send[mine]
    total[...] = jnp.zeros_like(total)
    if len(waves) > 1:
        pl.semaphore_wait(ready.at[0], 2)
    for step in range(1, len(waves) - 1):
        announce(step)
    if len(waves) > 1:
        send_tiles(1)
    for halo in yhalos:
        halo.wait()

    row = iota((cy, nz), 0)
    first_row, last_row = row == 0, row == cy - 1
    has_before, has_after = pencil > 0, pencil < n_pencil - 1

    def plane(x, sums):
        def ahead_y(c):
            edge = jnp.where(has_after, yhalo[1, c, pl.ds(x, 1), :], 0.0)
            return jnp.where(last_row, edge, pltpu.roll(field[c, x + 1], cy - 1, 0))

        def behind_y(c):
            edge = jnp.where(has_before, yhalo[0, c, pl.ds(x, 1), :], 0.0)
            return jnp.where(first_row, edge, pltpu.roll(field[c, x + 1], 1, 0))

        neighbours = [
            (lambda c: field[c, x + 2], lambda c: field[c, x]),
            (ahead_y, behind_y),
            (lambda c: pltpu.roll(field[c, x + 1], nz - 1, 1), lambda c: pltpu.roll(field[c, x + 1], 1, 1)),
        ]
        own = [field[c, x + 1] for c in range(3)]
        own_visc = field[6, x + 1]
        change = [jnp.zeros_like(own_visc) for c in range(3)]
        for d, (forward, backward) in enumerate(neighbours):
            factor = 0.5 * own[d]
            face_ahead = 0.5 * (own_visc + forward(6))
            face_behind = 0.5 * (own_visc + backward(6))
            for c in range(3):
                change[c] += factor * (forward(3 + c) - backward(3 + c))
                change[c] += face_ahead * (forward(c) - own[c])
                change[c] += face_behind * (backward(c) - own[c])
        result = []
        for c in range(3):
            value = own[c] + time_step * change[c]
            out[c, x] = value
            result.append(sums[c] + jnp.sum(value, axis=0, keepdims=True))
        return tuple(result)

    sums = lax.fori_loop(1, cx - 1, plane, tuple(jnp.zeros((1, nz), F32) for c in range(3)))
    for step in range(1, len(waves) - 1):
        pl.semaphore_wait(ready.at[step], 2)
        send_tiles(step + 1)
    for halo in xhalos:
        halo.wait()
    field[:, 0] = jnp.where(slab > 0, field[:, 0], 0.0)
    field[:, cx + 1] = jnp.where(slab < n_slab - 1, field[:, cx + 1], 0.0)
    sums = lax.fori_loop(0, 2, lambda i, sums: plane(i * (cx - 1), sums), sums)
    width = sums_in.shape[2]
    group = jnp.where(iota((nz, width), 0) // CB == iota((nz, width), 1) % levels, 1.0, 0.0)
    stacked = jnp.concatenate(list(sums) + [jnp.zeros((5, nz), F32)], axis=0)
    spread = jnp.dot(stacked, group, precision=HIGH, preferred_element_type=F32)
    sublane, lane = iota((8, width), 0), iota((8, width), 1)
    own_line = jnp.sum(jnp.where((lane // levels == sublane) & (sublane < 3), spread, 0.0), axis=0, keepdims=True)
    all_sums = remote(sums_send.at[1:NEAR], sums_in.at[1:NEAR], msend, mrecv, s_up)
    all_sums.wait_recv()
    message[...] = jnp.sum(sums_in[...], axis=0) + jnp.where(sublane == slab // NEAR, own_line, 0.0)
    far_first(1, n_slab - 1, lambda i: remote(message, everywhere.at[slab], bsend, brecv, slab_peer(i)).start())
    everywhere[slab] = message[...]
    gathered = remote(everywhere.at[1:n_slab], everywhere.at[1:n_slab], bsend, brecv, s_up)

    shape = (8, lanes)
    rel_x = [((slab - iota(shape, 0) * NEAR - x) * cx).astype(F32) for x in range(NEAR)]
    rel_y = ((iota(shape, 1) // levels - pencil) * cy).astype(F32)
    target_level = iota(shape, 1) % levels

    def rel_z(level):
        return ((target_level - level) * CB).astype(F32)

    def prepare(level, carry):
        along_z = rel_z(level)
        flat_sq = rel_y * rel_y + along_z * along_z + sigma * sigma
        for x in range(NEAR):
            inverse = lax.rsqrt(rel_x[x] * rel_x[x] + flat_sq)
            kern[level * NEAR + x] = inverse * inverse * inverse
        return carry

    lax.fori_loop(0, levels, prepare, 0)
    groups = tiles.shape[0] * 4 * tiles.shape[2] // lhs.shape[1]
    early = max(1, len(waves) - 1)
    for wave in range(early):
        tiles_of(wave).wait_recv()
    deposit(tiles, lhs, rhs, total, 0, groups // 2)
    for wave in range(early, len(waves)):
        tiles_of(wave).wait_recv()
    cut = groups * BEFORE // 8
    deposit(tiles, lhs, rhs, total, groups // 2, cut)

    gathered.wait_recv()
    moments = []
    for x in range(NEAR):
        rows = everywhere[x]
        for z in range(1, n_slab // NEAR):
            rows = rows + everywhere[z * NEAR + x]
        moments.append(rows)
    sums = [jnp.zeros(shape, F32) for c in range(3)]
    for level in range(levels):
        along_z = rel_z(level)
        for x in range(NEAR):
            m0, m1, m2 = (moments[x][:, c * levels + level : c * levels + level + 1] for c in range(3))
            weight = kern[level * NEAR + x]
            sums[0] += weight * (along_z * m1 - rel_y * m2)
            sums[1] += weight * (rel_x[x] * m2 - along_z * m0)
            sums[2] += weight * (rel_y * m0 - rel_x[x] * m1)
    lines = [jnp.sum(part, axis=0, keepdims=True) for part in sums]
    partial[...] = jnp.concatenate(lines + [jnp.zeros((5, lanes), F32)], axis=0)
    far_first(1, n_pencil - 1, lambda i: remote(partial, inbox.at[i], asend, arecv, pencil_peer(i)).start())
    inbox[0] = partial[...]
    arrived = remote(inbox.at[1:n_pencil], inbox.at[1:n_pencil], asend, arecv, p_up)

    deposit(tiles, lhs, rhs, total, cut, groups)
    stores = [pltpu.make_async_copy(out.at[c], out_hbm.at[c], out_sem.at[c]) for c in range(3)]
    for c in range(3):
        out[c] += total[c * cx * cy : (c + 1) * cx * cy].reshape(cx, cy, nz)
        stores[c].start()
    arrived.wait_recv()
    result = pltpu.roll(jnp.sum(inbox[...], axis=0), lax.rem(lanes - pencil * levels, lanes), 1)
    for c in range(3):
        far[c, 0] = result[c : c + 1, 0:levels]
    all_sums.wait_send()
    for wave in range(len(waves)):
        tiles_of(wave).wait_send()
    arrived.wait_send()
    gathered.wait_send()
    for store in stores:
        store.wait()


BEFORE = 5
NEAR = 4
GROUP = 4


def per_device(n_slab, n_pencil, vorticity, velocity, viscosity, tile_weights, tile_cells, tile_dest, tile_count):
    _, cx, cy, nz = vorticity.shape
    n_tiles, tile_len = tile_cells.shape
    levels = nz // CB
    lanes = n_pencil * levels
    hbm = pl.BlockSpec(memory_space=pltpu.HBM)
    vmem = pl.BlockSpec(memory_space=pltpu.VMEM)
    smem = pl.BlockSpec(memory_space=pltpu.SMEM)
    dma = pltpu.SemaphoreType.DMA
    outs = (jax.ShapeDtypeStruct(vorticity.shape, F32), jax.ShapeDtypeStruct((3, 1, 1, levels), F32))
    return pl.pallas_call(
        functools.partial(step_kernel, n_slab, n_pencil, float(cx * n_slab // 4)),
        out_shape=outs,
        in_specs=[hbm, hbm, hbm, hbm, hbm, vmem, smem],
        out_specs=(hbm, vmem),
        scratch_shapes=[
            pltpu.VMEM((FIELDS, cx + 2, cy, nz), F32),
            pltpu.VMEM((3, n_tiles, tile_len), F32),
            pltpu.VMEM((n_tiles, tile_len), jnp.int32),
            pltpu.VMEM((n_slab, 8, tile_len), F32),
            pltpu.VMEM((n_slab, 8, tile_len), F32),
            pltpu.VMEM((NEAR, 8, tile_len), F32),
            pltpu.VMEM((NEAR, 8, tile_len), F32),
            pltpu.VMEM((2, FIELDS, cx, nz), F32),
            pltpu.VMEM((2, FIELDS, cx, nz), F32),
            pltpu.VMEM((3 * cx * cy, GROUP * 4 * tile_len), BF16),
            pltpu.VMEM((nz, GROUP * 4 * tile_len), BF16),
            pltpu.VMEM((3 * cx * cy, nz), F32),
            pltpu.VMEM((3, cx, cy, nz), F32),
            pltpu.VMEM((8, tile_len), F32),
            pltpu.VMEM((n_slab, 8, tile_len), F32),
            pltpu.VMEM((levels * NEAR, 8, lanes), F32),
            pltpu.VMEM((8, lanes), F32),
            pltpu.VMEM((n_pencil, 8, lanes), F32),
            dma((5,)), dma((2,)), dma((2,)), dma((2,)), dma((2,)), dma((4,)), dma((4,)), dma, dma, dma, dma, dma, dma,
            pltpu.SemaphoreType.REGULAR((4,)), dma((3,)),
        ],
        compiler_params=pltpu.CompilerParams(collective_id=0, has_side_effects=True, vmem_limit_bytes=VMEM_LIMIT),
        name="step",
    )(
        vorticity, velocity, viscosity, jnp.transpose(tile_weights, (1, 0, 2)), tile_cells,
        tile_dest.reshape(1, -1), tile_count,
    )


def solution(mesh):
    in_specs = (
        P(None, "slab", "pencil", None),
        P(None, "slab", "pencil", None),
        P("slab", "pencil", None),
        P(("slab", "pencil"), None, None),
        P(("slab", "pencil"), None),
        P(("slab", "pencil"), None),
        P(("slab", "pencil")),
    )
    out_specs = (P(None, "slab", "pencil", None), P(None, "slab", "pencil", None))
    step = functools.partial(per_device, mesh.shape["slab"], mesh.shape["pencil"])
    return jax.shard_map(step, mesh=mesh, in_specs=in_specs, out_specs=out_specs, check_vma=False)
```

```python
import functools

import jax
import jax.numpy as jnp
from jax import lax
from jax.experimental import pallas as pl
from jax.experimental.pallas import tpu as pltpu
from jax.sharding import PartitionSpec as P

CB = 16
FIELDS = 7
time_step = 0.1
VMEM_LIMIT = 60 << 20
HIGH = lax.Precision.HIGHEST
F32 = jnp.float32
BF16 = jnp.bfloat16
MESH = pl.DeviceIdType.MESH


def iota(shape, dim):
    return lax.broadcasted_iota(jnp.int32, shape, dim)


def offset(i):
    return (2 * (i % 2) - 1) * ((i + 1) // 2)


def far_first(first, last, one):
    def body(j, carry):
        one(last - j)
        return carry

    lax.fori_loop(0, last - first + 1, body, 0)


def remote(src, dst, send_sem, recv_sem, device):
    return pltpu.make_async_remote_copy(
        src_ref=src, dst_ref=dst, send_sem=send_sem, recv_sem=recv_sem, device_id=device, device_id_type=MESH
    )


def pack_tiles(weights, cells, dest, live, send, sums, nz):
    n_slab = send.shape[0]
    tiles, lanes = cells.shape
    slab = iota((n_slab, tiles), 0)
    tile = iota((n_slab, tiles), 1)
    match = jnp.where((dest[...] == slab) & (tile < live), 1.0, 0.0)
    earlier = jnp.where(iota((tiles, tiles), 0) < iota((tiles, tiles), 1), 1.0, 0.0)
    before = jnp.dot(match, earlier, preferred_element_type=F32)
    for j in range(2):
        pick = jnp.where(before == j, match, 0.0)
        for c in range(4):
            rows = weights[c] if c < 3 else (cells[...] + 1).astype(F32)
            send[:, 4 * j + c, :] = jnp.dot(pick, rows, precision=HIGH, preferred_element_type=F32)
    levels = nz // CB
    level = (cells[...] & (nz - 1)) // CB
    lane = iota((tiles, lanes), 1)
    by_level = jnp.zeros((tiles, lanes), F32)
    for l in range(levels):
        here = level == l
        for c in range(3):
            total = jnp.sum(jnp.where(here, weights[c], 0.0), axis=1, keepdims=True)
            by_level = jnp.where(lane == c * levels + l, total, by_level)
    row = iota((NEAR * 8, tiles), 0)
    member = jnp.where(row % 8 < n_slab // NEAR, row % 8 * NEAR + row // 8, -1)
    match = jnp.where((dest[...] == member) & (iota((NEAR * 8, tiles), 1) < live), 1.0, 0.0)
    added = jnp.dot(match, by_level, precision=HIGH, preferred_element_type=F32)
    sums[...] = added.reshape(NEAR, 8, lanes)


def deposit(tiles, lhs, rhs, total, first, last):
    rows, nz = total.shape[0] // 3, total.shape[1]
    width = 2 * tiles.shape[2]
    group = lhs.shape[1] // (2 * width)
    shift = nz.bit_length() - 1
    number = iota((rows, width), 0).astype(F32).astype(BF16)
    one, zero = jnp.ones((), BF16), jnp.zeros((), BF16)

    def add(i, carry):
        for g in range(group):
            tile = tiles[i * group + g]
            entry = [jnp.concatenate([tile[c : c + 1], tile[4 + c : 5 + c]], axis=1) for c in range(4)]
            cell = entry[3].astype(jnp.int32) - 1
            high = (cell >> shift).astype(F32).astype(BF16)
            low = (cell & (nz - 1)).astype(F32).astype(BF16)
            here = number == high
            at = 2 * g * width
            for c in range(3):
                first_piece = entry[c].astype(BF16)
                second_piece = (entry[c] - first_piece.astype(F32)).astype(BF16)
                lhs[c * rows : (c + 1) * rows, at : at + width] = jnp.where(here, first_piece, zero)
                lhs[c * rows : (c + 1) * rows, at + width : at + 2 * width] = jnp.where(here, second_piece, zero)
            onehot = jnp.where(number == low, one, zero)
            rhs[:, at : at + width] = onehot
            rhs[:, at + width : at + 2 * width] = onehot
        total[...] += lax.dot_general(lhs[...], rhs[...], (((1,), (1,)), ((), ())), preferred_element_type=F32)
        return carry

    lax.fori_loop(first, last, add, 0)


def step_kernel(
    n_slab, n_pencil, sigma, vort, velo, visc, weights, cells, dest, count,
    out_hbm, far,
    field, wtile, ctile, send, tiles, sums_send, sums_in, yface, yhalo, lhs, rhs, total, out, message, everywhere, beside,
    kern, partial, inbox, load_sem, xsend, xrecv, xsend2, xrecv2, ysend, yrecv, tsend, trecv, msend, mrecv, asend, arecv, bsend, brecv, ready, out_sem,
):
    slab, pencil = lax.axis_index("slab"), lax.axis_index("pencil")
    cx, cy, nz = out.shape[1], out.shape[2], out.shape[3]
    lanes = partial.shape[1]
    levels = nz // CB
    waves = [min(2 * NEAR, n_slab - 1)]
    while waves[-1] < n_slab - 1:
        waves.append(min(2 * waves[-1], n_slab - 1))

    def slab_peer(i):
        return {"slab": lax.rem(slab + offset(i) + n_slab, n_slab)}

    def pencil_peer(i):
        return {"pencil": lax.rem(pencil + offset(i) + n_pencil, n_pencil)}

    loads = [
        pltpu.make_async_copy(vort, field.at[0:3, 1 : cx + 1], load_sem.at[0]),
        pltpu.make_async_copy(velo, field.at[3:6, 1 : cx + 1], load_sem.at[1]),
        pltpu.make_async_copy(visc, field.at[6, 1 : cx + 1], load_sem.at[2]),
    ]
    tile_loads = [
        pltpu.make_async_copy(weights, wtile, load_sem.at[3]),
        pltpu.make_async_copy(cells, ctile, load_sem.at[4]),
    ]
    for load in loads + tile_loads:
        load.start()
    barrier = pltpu.get_barrier_semaphore()

    def greet(where):
        pl.semaphore_signal(barrier, inc=1, device_id=where, device_id_type=MESH)

    far_first(1, waves[0], lambda i: greet(slab_peer(i)))
    far_first(1, n_pencil - 1, lambda i: greet(pencil_peer(i)))
    for load in loads:
        load.wait()
    for c in range(FIELDS):
        yface[0, c] = field[c, 1 : cx + 1, 0, :]
        yface[1, c] = field[c, 1 : cx + 1, cy - 1, :]
    pl.semaphore_wait(barrier, waves[0] + n_pencil - 1)

    s_up, s_down = slab_peer(1), slab_peer(2)
    p_up, p_down = pencil_peer(1), pencil_peer(2)
    yhalos = [
        remote(yface.at[0], yhalo.at[1], ysend.at[0], yrecv.at[1], p_down),
        remote(yface.at[1], yhalo.at[0], ysend.at[1], yrecv.at[0], p_up),
    ]
    low, high = slice(0, cy // 2), slice(cy // 2, cy)

    def face_halos(to_lower, to_upper, send_sem, recv_sem):
        return [
            remote(field.at[:, 1, to_lower], field.at[:, cx + 1, to_lower], send_sem.at[0], recv_sem.at[1], s_down),
            remote(field.at[:, cx, to_upper], field.at[:, 0, to_upper], send_sem.at[1], recv_sem.at[0], s_up),
        ]

    xhalos = face_halos(high, low, xsend, xrecv)
    xhalos2 = face_halos(low, high, xsend2, xrecv2)
    for halo in yhalos + xhalos:
        halo.start()

    def announce(step):
        for i in (waves[step] - 1, waves[step]):
            pl.semaphore_signal(ready.at[step], inc=1, device_id=slab_peer(i), device_id_type=MESH)

    def destination(i):
        return lax.rem(slab + offset(i) + n_slab, n_slab)

    def send_tiles(wave):
        first = 1 if wave == 0 else waves[wave - 1] + 1

        def one(i):
            remote(send.at[destination(i)], tiles.at[i], tsend.at[wave], trecv.at[wave], slab_peer(i)).start()

        far_first(first, waves[wave], one)

    def tiles_of(wave):
        first = 1 if wave == 0 else waves[wave - 1] + 1
        part = slice(first, waves[wave] + 1)
        return remote(send.at[part], tiles.at[part], tsend.at[wave], trecv.at[wave], s_up)

    if len(waves) > 1:
        announce(0)
    for load in tile_loads:
        load.wait()
    pack_tiles(wtile, ctile, dest, count[0], send, sums_send, nz)
    mine = lax.rem(slab, NEAR)

    def to_member(j):
        other = lax.rem(mine + j, NEAR)
        return remote(sums_send.at[other], sums_in.at[j], msend, mrecv, {"slab": slab - mine + other})

    for j in range(1, NEAR):
        to_member(j).start()
    send_tiles(0)
    tiles[0] = send[slab]
    sums_in[0] = sums_send[mine]
    total[...] = jnp.zeros_like(total)
    beside[...] = jnp.zeros_like(beside)
    if len(waves) > 1:
        pl.semaphore_wait(ready.at[0], 2)
    for step in range(1, len(waves) - 1):
        announce(step)
    if len(waves) > 1:
        send_tiles(1)
    for halo in yhalos:
        halo.wait()

    row = iota((cy, nz), 0)
    first_row, last_row = row == 0, row == cy - 1
    has_before, has_after = pencil > 0, pencil < n_pencil - 1

    def plane(x, sums, is_first=False, is_last=False):
        def ahead_y(c):
            edge = jnp.where(has_after, yhalo[1, c, pl.ds(x, 1), :], 0.0)
            return jnp.where(last_row, edge, pltpu.roll(field[c, x + 1], cy - 1, 0))

        def behind_y(c):
            edge = jnp.where(has_before, yhalo[0, c, pl.ds(x, 1), :], 0.0)
            return jnp.where(first_row, edge, pltpu.roll(field[c, x + 1], 1, 0))

        neighbours = [
            (
                (lambda c: 0.0) if is_last else (lambda c: field[c, x + 2]),
                (lambda c: 0.0) if is_first else (lambda c: field[c, x]),
            ),
            (ahead_y, behind_y),
            (lambda c: pltpu.roll(field[c, x + 1], nz - 1, 1), lambda c: pltpu.roll(field[c, x + 1], 1, 1)),
        ]
        own = [field[c, x + 1] for c in range(3)]
        own_visc = field[6, x + 1]
        change = [jnp.zeros_like(own_visc) for c in range(3)]
        for d, (forward, backward) in enumerate(neighbours):
            factor = 0.5 * own[d]
            face_ahead = 0.5 * (own_visc + forward(6))
            face_behind = 0.5 * (own_visc + backward(6))
            for c in range(3):
                change[c] += factor * (forward(3 + c) - backward(3 + c))
                if d > 0 or not is_last:
                    change[c] += face_ahead * (forward(c) - own[c])
                if d > 0 or not is_first:
                    change[c] += face_behind * (backward(c) - own[c])
        result = []
        for c in range(3):
            value = own[c] + time_step * change[c]
            out[c, x] = value
            result.append(sums[c] + jnp.sum(value, axis=0, keepdims=True))
        return tuple(result)

    def face(inner, outer, exists, sign, rows):
        here = [field[c, inner, rows] for c in range(FIELDS)]
        there = [jnp.where(exists, field[c, outer, rows], 0.0) for c in range(FIELDS)]
        middle = 0.5 * (here[6] + there[6])
        for_here, for_there = [], []
        for c in range(3):
            flow = middle * (there[c] - here[c])
            for_here.append(time_step * (sign * (0.5 * here[0]) * there[3 + c] + flow))
            for_there.append(jnp.where(exists, time_step * (-sign * (0.5 * there[0]) * here[3 + c] - flow), 0.0))
        return for_here, for_there

    def rim(inner, exists, rows):
        viscous = 0.5 * time_step * field[6, inner, rows]
        return [jnp.where(exists, 0.0, -viscous * field[c, inner, rows]) for c in range(3)]

    def over_rows(values):
        return [jnp.sum(value, axis=0, keepdims=True) for value in values]

    sums = lax.fori_loop(1, cx - 1, plane, tuple(jnp.zeros((1, nz), F32) for c in range(3)))
    sums = plane(0, sums, is_first=True)
    sums = plane(cx - 1, sums, is_last=True)
    has_lower, has_upper = slab > 0, slab < n_slab - 1
    rims = [over_rows(rim(1, has_lower, high)), over_rows(rim(cx, has_upper, low))]
    sums = [sums[c] + rims[0][c] + rims[1][c] for c in range(3)]
    for step in range(1, len(waves) - 1):
        pl.semaphore_wait(ready.at[step], 2)
        send_tiles(step + 1)
    for halo in xhalos:
        halo.wait()
    lower_own, lower_other = map(over_rows, face(1, 0, has_lower, -1.0, low))
    upper_own, upper_other = map(over_rows, face(cx, cx + 1, has_upper, 1.0, high))
    sums = [sums[c] + lower_own[c] + upper_own[c] for c in range(3)]
    width = sums_in.shape[2]
    group = jnp.where(iota((nz, width), 0) // CB == iota((nz, width), 1) % levels, 1.0, 0.0)
    stacked = jnp.concatenate(sums + upper_other + lower_other + [jnp.zeros((7, nz), F32)], axis=0)
    spread = jnp.dot(stacked, group, precision=HIGH, preferred_element_type=F32)
    sublane, lane = iota((16, width), 0), iota((16, width), 1)
    part, third = lane // levels % 4, lane // (width // 2)

    def line(mask):
        return jnp.sum(jnp.where(mask, spread, 0.0), axis=0, keepdims=True)

    own_line = line((third == 0) & (part < 3) & (sublane == part))
    beside_line = line((part < 3) & (sublane == 3 + 3 * third + part))
    all_sums = remote(sums_send.at[1:NEAR], sums_in.at[1:NEAR], msend, mrecv, s_up)
    all_sums.wait_recv()
    rows = jnp.sum(sums_in[...], axis=0) + jnp.where(iota((8, width), 0) == slab // NEAR, own_line, 0.0)
    message[0:4] = rows[0:4] + pltpu.roll(rows, width // 2, 1)[4:8]
    message[4:5] = beside_line
    far_first(
        1, n_slab - 1,
        lambda i: remote(message.at[0:5], everywhere.at[slab, 0:5], bsend, brecv, slab_peer(i)).start(),
    )
    for halo in xhalos2:
        halo.start()
    everywhere[slab, 0:5] = message[0:5]
    gathered = remote(everywhere.at[1:n_slab, 0:5], everywhere.at[1:n_slab, 0:5], bsend, brecv, s_up)

    shape = (8, lanes)
    rel_x = [((slab - iota(shape, 0) * NEAR - x) * cx).astype(F32) for x in range(NEAR)]
    rel_y = ((iota(shape, 1) // levels - pencil) * cy).astype(F32)
    target_level = iota(shape, 1) % levels

    def rel_z(level):
        return ((target_level - level) * CB).astype(F32)

    def prepare(level, carry):
        along_z = rel_z(level)
        flat_sq = rel_y * rel_y + along_z * along_z + sigma * sigma
        for x in range(NEAR):
            inverse = lax.rsqrt(rel_x[x] * rel_x[x] + flat_sq)
            kern[level * NEAR + x] = inverse * inverse * inverse
        return carry

    lax.fori_loop(0, levels, prepare, 0)
    groups = tiles.shape[0] * 4 * tiles.shape[2] // lhs.shape[1]
    early = max(1, len(waves) - 1)
    for wave in range(early):
        tiles_of(wave).wait_recv()
    deposit(tiles, lhs, rhs, total, 0, groups // 2)
    for wave in range(early, len(waves)):
        tiles_of(wave).wait_recv()
    cut = groups * BEFORE // 8
    deposit(tiles, lhs, rhs, total, groups // 2, cut)

    gathered.wait_recv()
    beside[8 : 8 + n_slab, :] = everywhere[:, 4, :]
    moments = []
    for x in range(NEAR):
        rows = everywhere[x, 0:4]
        for z in range(1, n_slab // NEAR):
            rows = rows + everywhere[z * NEAR + x, 0:4]
        rows = jnp.concatenate([rows, pltpu.roll(rows, width // 2, 1)], axis=0)
        from_lower = beside[pl.ds(7 + x, 8, stride=NEAR), :]
        from_upper = beside[pl.ds(9 + x, 8, stride=NEAR), :]
        moments.append(rows + from_lower + pltpu.roll(from_upper, width // 2, 1))
    sums = [jnp.zeros(shape, F32) for c in range(3)]
    for level in range(levels):
        along_z = rel_z(level)
        for x in range(NEAR):
            m0, m1, m2 = (moments[x][:, c * levels + level : c * levels + level + 1] for c in range(3))
            weight = kern[level * NEAR + x]
            sums[0] += weight * (along_z * m1 - rel_y * m2)
            sums[1] += weight * (rel_x[x] * m2 - along_z * m0)
            sums[2] += weight * (rel_y * m0 - rel_x[x] * m1)
    lines = [jnp.sum(part, axis=0, keepdims=True) for part in sums]
    partial[...] = jnp.concatenate(lines + [jnp.zeros((5, lanes), F32)], axis=0)
    far_first(1, n_pencil - 1, lambda i: remote(partial, inbox.at[i], asend, arecv, pencil_peer(i)).start())
    inbox[0] = partial[...]
    arrived = remote(inbox.at[1:n_pencil], inbox.at[1:n_pencil], asend, arecv, p_up)

    deposit(tiles, lhs, rhs, total, cut, groups)
    for halo in xhalos2:
        halo.wait()
    everything = slice(0, cy)
    for x, inner, outer, exists, sign in ((0, 1, 0, has_lower, -1.0), (cx - 1, cx, cx + 1, has_upper, 1.0)):
        terms, _ = face(inner, outer, exists, sign, everything)
        for c in range(3):
            out[c, x] += terms[c]
    stores = [pltpu.make_async_copy(out.at[c], out_hbm.at[c], out_sem.at[c]) for c in range(3)]
    for c in range(3):
        out[c] += total[c * cx * cy : (c + 1) * cx * cy].reshape(cx, cy, nz)
        stores[c].start()
    arrived.wait_recv()
    result = pltpu.roll(jnp.sum(inbox[...], axis=0), lax.rem(lanes - pencil * levels, lanes), 1)
    for c in range(3):
        far[c, 0] = result[c : c + 1, 0:levels]
    all_sums.wait_send()
    for wave in range(len(waves)):
        tiles_of(wave).wait_send()
    arrived.wait_send()
    gathered.wait_send()
    for store in stores:
        store.wait()


BEFORE = 5
NEAR = 4
GROUP = 4


def per_device(n_slab, n_pencil, vorticity, velocity, viscosity, tile_weights, tile_cells, tile_dest, tile_count):
    _, cx, cy, nz = vorticity.shape
    n_tiles, tile_len = tile_cells.shape
    levels = nz // CB
    lanes = n_pencil * levels
    hbm = pl.BlockSpec(memory_space=pltpu.HBM)
    vmem = pl.BlockSpec(memory_space=pltpu.VMEM)
    smem = pl.BlockSpec(memory_space=pltpu.SMEM)
    dma = pltpu.SemaphoreType.DMA
    outs = (jax.ShapeDtypeStruct(vorticity.shape, F32), jax.ShapeDtypeStruct((3, 1, 1, levels), F32))
    return pl.pallas_call(
        functools.partial(step_kernel, n_slab, n_pencil, float(cx * n_slab // 4)),
        out_shape=outs,
        in_specs=[hbm, hbm, hbm, hbm, hbm, vmem, smem],
        out_specs=(hbm, vmem),
        scratch_shapes=[
            pltpu.VMEM((FIELDS, cx + 2, cy, nz), F32),
            pltpu.VMEM((3, n_tiles, tile_len), F32),
            pltpu.VMEM((n_tiles, tile_len), jnp.int32),
            pltpu.VMEM((n_slab, 8, tile_len), F32),
            pltpu.VMEM((n_slab, 8, tile_len), F32),
            pltpu.VMEM((NEAR, 8, tile_len), F32),
            pltpu.VMEM((NEAR, 8, tile_len), F32),
            pltpu.VMEM((2, FIELDS, cx, nz), F32),
            pltpu.VMEM((2, FIELDS, cx, nz), F32),
            pltpu.VMEM((3 * cx * cy, GROUP * 4 * tile_len), BF16),
            pltpu.VMEM((nz, GROUP * 4 * tile_len), BF16),
            pltpu.VMEM((3 * cx * cy, nz), F32),
            pltpu.VMEM((3, cx, cy, nz), F32),
            pltpu.VMEM((8, tile_len), F32),
            pltpu.VMEM((n_slab, 8, tile_len), F32),
            pltpu.VMEM((8 * NEAR + 16, tile_len), F32),
            pltpu.VMEM((levels * NEAR, 8, lanes), F32),
            pltpu.VMEM((8, lanes), F32),
            pltpu.VMEM((n_pencil, 8, lanes), F32),
            dma((5,)), dma((2,)), dma((2,)), dma((2,)), dma((2,)), dma((2,)), dma((2,)), dma((4,)), dma((4,)), dma, dma, dma, dma, dma, dma,
            pltpu.SemaphoreType.REGULAR((4,)), dma((3,)),
        ],
        compiler_params=pltpu.CompilerParams(collective_id=0, has_side_effects=True, vmem_limit_bytes=VMEM_LIMIT),
        name="step",
    )(
        vorticity, velocity, viscosity, jnp.transpose(tile_weights, (1, 0, 2)), tile_cells,
        tile_dest.reshape(1, -1), tile_count,
    )


def solution(mesh):
    in_specs = (
        P(None, "slab", "pencil", None),
        P(None, "slab", "pencil", None),
        P("slab", "pencil", None),
        P(("slab", "pencil"), None, None),
        P(("slab", "pencil"), None),
        P(("slab", "pencil"), None),
        P(("slab", "pencil")),
    )
    out_specs = (P(None, "slab", "pencil", None), P(None, "slab", "pencil", None))
    step = functools.partial(per_device, mesh.shape["slab"], mesh.shape["pencil"])
    return jax.shard_map(step, mesh=mesh, in_specs=in_specs, out_specs=out_specs, check_vma=False)
```

```python
import functools

import jax
import jax.numpy as jnp
from jax import lax
from jax.experimental import pallas as pl
from jax.experimental.pallas import tpu as pltpu
from jax.sharding import PartitionSpec as P

CB = 16
FIELDS = 7
time_step = 0.1
VMEM_LIMIT = 60 << 20
HIGH = lax.Precision.HIGHEST
F32 = jnp.float32
BF16 = jnp.bfloat16
MESH = pl.DeviceIdType.MESH


def iota(shape, dim):
    return lax.broadcasted_iota(jnp.int32, shape, dim)


def offset(i):
    return (2 * (i % 2) - 1) * ((i + 1) // 2)


def far_first(first, last, one):
    def body(j, carry):
        one(last - j)
        return carry

    lax.fori_loop(0, last - first + 1, body, 0)


def remote(src, dst, send_sem, recv_sem, device):
    return pltpu.make_async_remote_copy(
        src_ref=src, dst_ref=dst, send_sem=send_sem, recv_sem=recv_sem, device_id=device, device_id_type=MESH
    )


def pack_tiles(weights, cells, dest, live, send, sums, nz):
    n_slab = send.shape[0]
    tiles, lanes = cells.shape
    slab = iota((n_slab, tiles), 0)
    tile = iota((n_slab, tiles), 1)
    match = jnp.where((dest[...] == slab) & (tile < live), 1.0, 0.0)
    earlier = jnp.where(iota((tiles, tiles), 0) < iota((tiles, tiles), 1), 1.0, 0.0)
    before = jnp.dot(match, earlier, preferred_element_type=F32)
    for j in range(2):
        pick = jnp.where(before == j, match, 0.0)
        for c in range(4):
            rows = weights[c] if c < 3 else (cells[...] + 1).astype(F32)
            send[:, 4 * j + c, :] = jnp.dot(pick, rows, precision=HIGH, preferred_element_type=F32)
    levels = nz // CB
    level = (cells[...] & (nz - 1)) // CB
    lane = iota((tiles, lanes), 1)
    by_level = jnp.zeros((tiles, lanes), F32)
    for l in range(levels):
        here = level == l
        for c in range(3):
            total = jnp.sum(jnp.where(here, weights[c], 0.0), axis=1, keepdims=True)
            by_level = jnp.where(lane == c * levels + l, total, by_level)
    row = iota((NEAR * 8, tiles), 0)
    member = jnp.where(row % 8 < n_slab // NEAR, row % 8 * NEAR + row // 8, -1)
    match = jnp.where((dest[...] == member) & (iota((NEAR * 8, tiles), 1) < live), 1.0, 0.0)
    added = jnp.dot(match, by_level, precision=HIGH, preferred_element_type=F32)
    sums[...] = added.reshape(NEAR, 8, lanes)


def deposit(tiles, lhs, rhs, total, first, last):
    rows, nz = total.shape[0] // 3, total.shape[1]
    width = 2 * tiles.shape[2]
    group = lhs.shape[1] // (2 * width)
    shift = nz.bit_length() - 1
    number = iota((rows, width), 0).astype(F32).astype(BF16)
    one, zero = jnp.ones((), BF16), jnp.zeros((), BF16)

    def add(i, carry):
        for g in range(group):
            tile = tiles[i * group + g]
            entry = [jnp.concatenate([tile[c : c + 1], tile[4 + c : 5 + c]], axis=1) for c in range(4)]
            cell = entry[3].astype(jnp.int32) - 1
            high = (cell >> shift).astype(F32).astype(BF16)
            low = (cell & (nz - 1)).astype(F32).astype(BF16)
            here = number == high
            at = 2 * g * width
            for c in range(3):
                first_piece = entry[c].astype(BF16)
                second_piece = (entry[c] - first_piece.astype(F32)).astype(BF16)
                lhs[c * rows : (c + 1) * rows, at : at + width] = jnp.where(here, first_piece, zero)
                lhs[c * rows : (c + 1) * rows, at + width : at + 2 * width] = jnp.where(here, second_piece, zero)
            onehot = jnp.where(number == low, one, zero)
            rhs[:, at : at + width] = onehot
            rhs[:, at + width : at + 2 * width] = onehot
        total[...] += lax.dot_general(lhs[...], rhs[...], (((1,), (1,)), ((), ())), preferred_element_type=F32)
        return carry

    lax.fori_loop(first, last, add, 0)


def step_kernel(
    n_slab, n_pencil, sigma, vort, velo, visc, weights, cells, dest, count,
    out_hbm, far,
    field, wtile, ctile, send, tiles, sums_send, sums_in, yface, yhalo, lhs, rhs, total, out, message, everywhere, beside,
    kern, partial, inbox, load_sem, xsend, xrecv, xsend2, xrecv2, ysend, yrecv, tsend, trecv, msend, mrecv, asend, arecv, bsend, brecv, ready, out_sem,
):
    slab, pencil = lax.axis_index("slab"), lax.axis_index("pencil")
    cx, cy, nz = out.shape[1], out.shape[2], out.shape[3]
    lanes = partial.shape[1]
    levels = nz // CB
    waves = [min(2 * GREET, n_slab - 1)]
    while waves[-1] < n_slab - 1:
        waves.append(min(2 * waves[-1], n_slab - 1))

    def slab_peer(i):
        return {"slab": lax.rem(slab + offset(i) + n_slab, n_slab)}

    def pencil_peer(i):
        return {"pencil": lax.rem(pencil + offset(i) + n_pencil, n_pencil)}

    loads = [
        pltpu.make_async_copy(vort, field.at[0:3, 1 : cx + 1], load_sem.at[0]),
        pltpu.make_async_copy(velo, field.at[3:6, 1 : cx + 1], load_sem.at[1]),
        pltpu.make_async_copy(visc, field.at[6, 1 : cx + 1], load_sem.at[2]),
    ]
    tile_loads = [
        pltpu.make_async_copy(weights, wtile, load_sem.at[3]),
        pltpu.make_async_copy(cells, ctile, load_sem.at[4]),
    ]
    for load in loads + tile_loads:
        load.start()
    barrier = pltpu.get_barrier_semaphore()

    def greet(where):
        pl.semaphore_signal(barrier, inc=1, device_id=where, device_id_type=MESH)

    far_first(1, waves[0], lambda i: greet(slab_peer(i)))
    far_first(1, n_pencil - 1, lambda i: greet(pencil_peer(i)))
    for load in loads:
        load.wait()
    for c in range(FIELDS):
        yface[0, c] = field[c, 1 : cx + 1, 0, :]
        yface[1, c] = field[c, 1 : cx + 1, cy - 1, :]
    pl.semaphore_wait(barrier, waves[0] + n_pencil - 1)

    s_up, s_down = slab_peer(1), slab_peer(2)
    p_up, p_down = pencil_peer(1), pencil_peer(2)
    yhalos = [
        remote(yface.at[0], yhalo.at[1], ysend.at[0], yrecv.at[1], p_down),
        remote(yface.at[1], yhalo.at[0], ysend.at[1], yrecv.at[0], p_up),
    ]
    low, high = slice(0, cy // 2), slice(cy // 2, cy)

    def face_halos(to_lower, to_upper, send_sem, recv_sem):
        return [
            remote(field.at[:, 1, to_lower], field.at[:, cx + 1, to_lower], send_sem.at[0], recv_sem.at[1], s_down),
            remote(field.at[:, cx, to_upper], field.at[:, 0, to_upper], send_sem.at[1], recv_sem.at[0], s_up),
        ]

    xhalos = face_halos(high, low, xsend, xrecv)
    xhalos2 = face_halos(low, high, xsend2, xrecv2)
    for halo in yhalos + xhalos:
        halo.start()

    def announce(step):
        for i in (waves[step] - 1, waves[step]):
            pl.semaphore_signal(ready.at[step], inc=1, device_id=slab_peer(i), device_id_type=MESH)

    def destination(i):
        return lax.rem(slab + offset(i) + n_slab, n_slab)

    def send_tiles(wave):
        first = 1 if wave == 0 else waves[wave - 1] + 1

        def one(i):
            remote(send.at[destination(i)], tiles.at[i], tsend.at[wave], trecv.at[wave], slab_peer(i)).start()

        far_first(first, waves[wave], one)

    def tiles_of(wave):
        first = 1 if wave == 0 else waves[wave - 1] + 1
        part = slice(first, waves[wave] + 1)
        return remote(send.at[part], tiles.at[part], tsend.at[wave], trecv.at[wave], s_up)

    if len(waves) > 1:
        announce(0)
    for load in tile_loads:
        load.wait()
    pack_tiles(wtile, ctile, dest, count[0], send, sums_send, nz)
    mine = lax.rem(slab, NEAR)

    def to_member(j):
        other = lax.rem(mine + j, NEAR)
        return remote(sums_send.at[other], sums_in.at[j], msend, mrecv, {"slab": slab - mine + other})

    for j in range(1, NEAR):
        to_member(j).start()
    send_tiles(0)
    tiles[0] = send[slab]
    sums_in[0] = sums_send[mine]
    total[...] = jnp.zeros_like(total)
    beside[...] = jnp.zeros_like(beside)
    for step in range(1, len(waves) - 1):
        pl.semaphore_wait(ready.at[step - 1], 2)
        announce(step)
        send_tiles(step)
    for halo in yhalos:
        halo.wait()

    row = iota((cy, nz), 0)
    first_row, last_row = row == 0, row == cy - 1
    has_before, has_after = pencil > 0, pencil < n_pencil - 1

    def plane(x, sums, is_first=False, is_last=False):
        def ahead_y(c):
            edge = jnp.where(has_after, yhalo[1, c, pl.ds(x, 1), :], 0.0)
            return jnp.where(last_row, edge, pltpu.roll(field[c, x + 1], cy - 1, 0))

        def behind_y(c):
            edge = jnp.where(has_before, yhalo[0, c, pl.ds(x, 1), :], 0.0)
            return jnp.where(first_row, edge, pltpu.roll(field[c, x + 1], 1, 0))

        neighbours = [
            (
                (lambda c: 0.0) if is_last else (lambda c: field[c, x + 2]),
                (lambda c: 0.0) if is_first else (lambda c: field[c, x]),
            ),
            (ahead_y, behind_y),
            (lambda c: pltpu.roll(field[c, x + 1], nz - 1, 1), lambda c: pltpu.roll(field[c, x + 1], 1, 1)),
        ]
        own = [field[c, x + 1] for c in range(3)]
        own_visc = field[6, x + 1]
        change = [jnp.zeros_like(own_visc) for c in range(3)]
        for d, (forward, backward) in enumerate(neighbours):
            factor = 0.5 * own[d]
            face_ahead = 0.5 * (own_visc + forward(6))
            face_behind = 0.5 * (own_visc + backward(6))
            for c in range(3):
                change[c] += factor * (forward(3 + c) - backward(3 + c))
                if d > 0 or not is_last:
                    change[c] += face_ahead * (forward(c) - own[c])
                if d > 0 or not is_first:
                    change[c] += face_behind * (backward(c) - own[c])
        result = []
        for c in range(3):
            value = own[c] + time_step * change[c]
            out[c, x] = value
            result.append(sums[c] + jnp.sum(value, axis=0, keepdims=True))
        return tuple(result)

    def face(inner, outer, exists, sign, rows):
        here = [field[c, inner, rows] for c in range(FIELDS)]
        there = [jnp.where(exists, field[c, outer, rows], 0.0) for c in range(FIELDS)]
        middle = 0.5 * (here[6] + there[6])
        for_here, for_there = [], []
        for c in range(3):
            flow = middle * (there[c] - here[c])
            for_here.append(time_step * (sign * (0.5 * here[0]) * there[3 + c] + flow))
            for_there.append(jnp.where(exists, time_step * (-sign * (0.5 * there[0]) * here[3 + c] - flow), 0.0))
        return for_here, for_there

    def rim(inner, exists, rows):
        viscous = 0.5 * time_step * field[6, inner, rows]
        return [jnp.where(exists, 0.0, -viscous * field[c, inner, rows]) for c in range(3)]

    def over_rows(values):
        return [jnp.sum(value, axis=0, keepdims=True) for value in values]

    sums = lax.fori_loop(1, SPLIT, plane, tuple(jnp.zeros((1, nz), F32) for c in range(3)))
    if len(waves) > 1:
        pl.semaphore_wait(ready.at[len(waves) - 2], 2)
        send_tiles(len(waves) - 1)
    sums = lax.fori_loop(SPLIT, cx - 1, plane, sums)
    sums = plane(0, sums, is_first=True)
    sums = plane(cx - 1, sums, is_last=True)
    has_lower, has_upper = slab > 0, slab < n_slab - 1
    rims = [over_rows(rim(1, has_lower, high)), over_rows(rim(cx, has_upper, low))]
    sums = [sums[c] + rims[0][c] + rims[1][c] for c in range(3)]
    for halo in xhalos:
        halo.wait()
    lower_own, lower_other = map(over_rows, face(1, 0, has_lower, -1.0, low))
    upper_own, upper_other = map(over_rows, face(cx, cx + 1, has_upper, 1.0, high))
    sums = [sums[c] + lower_own[c] + upper_own[c] for c in range(3)]
    width = sums_in.shape[2]
    group = jnp.where(iota((nz, width), 0) // CB == iota((nz, width), 1) % levels, 1.0, 0.0)
    stacked = jnp.concatenate(sums + upper_other + lower_other + [jnp.zeros((7, nz), F32)], axis=0)
    spread = jnp.dot(stacked, group, precision=HIGH, preferred_element_type=F32)
    sublane, lane = iota((16, width), 0), iota((16, width), 1)
    part, third = lane // levels % 4, lane // (width // 2)

    def line(mask):
        return jnp.sum(jnp.where(mask, spread, 0.0), axis=0, keepdims=True)

    own_line = line((third == 0) & (part < 3) & (sublane == part))
    beside_line = line((part < 3) & (sublane == 3 + 3 * third + part))
    all_sums = remote(sums_send.at[1:NEAR], sums_in.at[1:NEAR], msend, mrecv, s_up)
    all_sums.wait_recv()
    rows = jnp.sum(sums_in[...], axis=0) + jnp.where(iota((8, width), 0) == slab // NEAR, own_line, 0.0)
    message[0:4] = rows[0:4] + pltpu.roll(rows, width // 2, 1)[4:8]
    message[4:5] = beside_line
    far_first(
        1, n_slab - 1,
        lambda i: remote(message.at[0:5], everywhere.at[slab, 0:5], bsend, brecv, slab_peer(i)).start(),
    )
    for halo in xhalos2:
        halo.start()
    everywhere[slab, 0:5] = message[0:5]
    gathered = remote(everywhere.at[1:n_slab, 0:5], everywhere.at[1:n_slab, 0:5], bsend, brecv, s_up)

    shape = (8, lanes)
    rel_x = [((slab - iota(shape, 0) * NEAR - x) * cx).astype(F32) for x in range(NEAR)]
    rel_y = ((iota(shape, 1) // levels - pencil) * cy).astype(F32)
    target_level = iota(shape, 1) % levels

    def rel_z(level):
        return ((target_level - level) * CB).astype(F32)

    def prepare(level, carry):
        along_z = rel_z(level)
        flat_sq = rel_y * rel_y + along_z * along_z + sigma * sigma
        for x in range(NEAR):
            inverse = lax.rsqrt(rel_x[x] * rel_x[x] + flat_sq)
            kern[level * NEAR + x] = inverse * inverse * inverse
        return carry

    lax.fori_loop(0, levels, prepare, 0)
    groups = tiles.shape[0] * 4 * tiles.shape[2] // lhs.shape[1]
    early = max(1, len(waves) - 1)
    for wave in range(early):
        tiles_of(wave).wait_recv()
    deposit(tiles, lhs, rhs, total, 0, groups // 2)
    for wave in range(early, len(waves)):
        tiles_of(wave).wait_recv()
    cut = groups * BEFORE // 8
    deposit(tiles, lhs, rhs, total, groups // 2, cut)

    gathered.wait_recv()
    beside[8 : 8 + n_slab, :] = everywhere[:, 4, :]
    moments = []
    for x in range(NEAR):
        rows = everywhere[x, 0:4]
        for z in range(1, n_slab // NEAR):
            rows = rows + everywhere[z * NEAR + x, 0:4]
        rows = jnp.concatenate([rows, pltpu.roll(rows, width // 2, 1)], axis=0)
        from_lower = beside[pl.ds(7 + x, 8, stride=NEAR), :]
        from_upper = beside[pl.ds(9 + x, 8, stride=NEAR), :]
        moments.append(rows + from_lower + pltpu.roll(from_upper, width // 2, 1))
    sums = [jnp.zeros(shape, F32) for c in range(3)]
    for level in range(levels):
        along_z = rel_z(level)
        for x in range(NEAR):
            m0, m1, m2 = (moments[x][:, c * levels + level : c * levels + level + 1] for c in range(3))
            weight = kern[level * NEAR + x]
            sums[0] += weight * (along_z * m1 - rel_y * m2)
            sums[1] += weight * (rel_x[x] * m2 - along_z * m0)
            sums[2] += weight * (rel_y * m0 - rel_x[x] * m1)
    lines = [jnp.sum(part, axis=0, keepdims=True) for part in sums]
    partial[0:4] = jnp.concatenate(lines + [jnp.zeros((1, lanes), F32)], axis=0)
    far_first(1, n_pencil - 1, lambda i: remote(partial.at[0:4], inbox.at[i, 0:4], asend, arecv, pencil_peer(i)).start())
    inbox[0, 0:4] = partial[0:4]
    arrived = remote(inbox.at[1:n_pencil, 0:4], inbox.at[1:n_pencil, 0:4], asend, arecv, p_up)

    deposit(tiles, lhs, rhs, total, cut, groups)
    for halo in xhalos2:
        halo.wait()
    everything = slice(0, cy)
    for x, inner, outer, exists, sign in ((0, 1, 0, has_lower, -1.0), (cx - 1, cx, cx + 1, has_upper, 1.0)):
        terms, _ = face(inner, outer, exists, sign, everything)
        for c in range(3):
            out[c, x] += terms[c]
    stores = [pltpu.make_async_copy(out.at[c], out_hbm.at[c], out_sem.at[c]) for c in range(3)]
    for c in range(3):
        out[c] += total[c * cx * cy : (c + 1) * cx * cy].reshape(cx, cy, nz)
        stores[c].start()
    arrived.wait_recv()
    result = pltpu.roll(jnp.sum(inbox[:, 0:4, :], axis=0), lax.rem(lanes - pencil * levels, lanes), 1)
    for c in range(3):
        far[c, 0] = result[c : c + 1, 0:levels]
    all_sums.wait_send()
    for wave in range(len(waves)):
        tiles_of(wave).wait_send()
    arrived.wait_send()
    gathered.wait_send()
    for store in stores:
        store.wait()


BEFORE = 5
NEAR = 4
GREET = 4
SPLIT = 4
GROUP = 4


def per_device(n_slab, n_pencil, vorticity, velocity, viscosity, tile_weights, tile_cells, tile_dest, tile_count):
    _, cx, cy, nz = vorticity.shape
    n_tiles, tile_len = tile_cells.shape
    levels = nz // CB
    lanes = n_pencil * levels
    hbm = pl.BlockSpec(memory_space=pltpu.HBM)
    vmem = pl.BlockSpec(memory_space=pltpu.VMEM)
    smem = pl.BlockSpec(memory_space=pltpu.SMEM)
    dma = pltpu.SemaphoreType.DMA
    outs = (jax.ShapeDtypeStruct(vorticity.shape, F32), jax.ShapeDtypeStruct((3, 1, 1, levels), F32))
    return pl.pallas_call(
        functools.partial(step_kernel, n_slab, n_pencil, float(cx * n_slab // 4)),
        out_shape=outs,
        in_specs=[hbm, hbm, hbm, hbm, hbm, vmem, smem],
        out_specs=(hbm, vmem),
        scratch_shapes=[
            pltpu.VMEM((FIELDS, cx + 2, cy, nz), F32),
            pltpu.VMEM((3, n_tiles, tile_len), F32),
            pltpu.VMEM((n_tiles, tile_len), jnp.int32),
            pltpu.VMEM((n_slab, 8, tile_len), F32),
            pltpu.VMEM((n_slab, 8, tile_len), F32),
            pltpu.VMEM((NEAR, 8, tile_len), F32),
            pltpu.VMEM((NEAR, 8, tile_len), F32),
            pltpu.VMEM((2, FIELDS, cx, nz), F32),
            pltpu.VMEM((2, FIELDS, cx, nz), F32),
            pltpu.VMEM((3 * cx * cy, GROUP * 4 * tile_len), BF16),
            pltpu.VMEM((nz, GROUP * 4 * tile_len), BF16),
            pltpu.VMEM((3 * cx * cy, nz), F32),
            pltpu.VMEM((3, cx, cy, nz), F32),
            pltpu.VMEM((8, tile_len), F32),
            pltpu.VMEM((n_slab, 8, tile_len), F32),
            pltpu.VMEM((8 * NEAR + 16, tile_len), F32),
            pltpu.VMEM((levels * NEAR, 8, lanes), F32),
            pltpu.VMEM((8, lanes), F32),
            pltpu.VMEM((n_pencil, 8, lanes), F32),
            dma((5,)), dma((2,)), dma((2,)), dma((2,)), dma((2,)), dma((2,)), dma((2,)), dma((4,)), dma((4,)), dma, dma, dma, dma, dma, dma,
            pltpu.SemaphoreType.REGULAR((4,)), dma((3,)),
        ],
        compiler_params=pltpu.CompilerParams(collective_id=0, has_side_effects=True, vmem_limit_bytes=VMEM_LIMIT),
        name="step",
    )(
        vorticity, velocity, viscosity, jnp.transpose(tile_weights, (1, 0, 2)), tile_cells,
        tile_dest.reshape(1, -1), tile_count,
    )


def solution(mesh):
    in_specs = (
        P(None, "slab", "pencil", None),
        P(None, "slab", "pencil", None),
        P("slab", "pencil", None),
        P(("slab", "pencil"), None, None),
        P(("slab", "pencil"), None),
        P(("slab", "pencil"), None),
        P(("slab", "pencil")),
    )
    out_specs = (P(None, "slab", "pencil", None), P(None, "slab", "pencil", None))
    step = functools.partial(per_device, mesh.shape["slab"], mesh.shape["pencil"])
    return jax.shard_map(step, mesh=mesh, in_specs=in_specs, out_specs=out_specs, check_vma=False)
```

```python
import functools

import jax
import jax.numpy as jnp
from jax import lax
from jax.experimental import pallas as pl
from jax.experimental.pallas import tpu as pltpu
from jax.sharding import PartitionSpec as P

CB = 16
FIELDS = 7
time_step = 0.1
VMEM_LIMIT = 60 << 20
HIGH = lax.Precision.HIGHEST
F32 = jnp.float32
BF16 = jnp.bfloat16
MESH = pl.DeviceIdType.MESH


def iota(shape, dim):
    return lax.broadcasted_iota(jnp.int32, shape, dim)


def offset(i):
    return (2 * (i % 2) - 1) * ((i + 1) // 2)


def far_first(first, last, one):
    def body(j, carry):
        one(last - j)
        return carry

    lax.fori_loop(0, last - first + 1, body, 0)


def remote(src, dst, send_sem, recv_sem, device):
    return pltpu.make_async_remote_copy(
        src_ref=src, dst_ref=dst, send_sem=send_sem, recv_sem=recv_sem, device_id=device, device_id_type=MESH
    )


def pieces(values):
    first = values.astype(BF16)
    rest = values - first.astype(F32)
    second = rest.astype(BF16)
    return [first, second, (rest - second.astype(F32)).astype(BF16)]


def pick_dot(ones, values):
    width = values.shape[1]
    wide = jnp.dot(ones.astype(BF16), jnp.concatenate(pieces(values), axis=1), preferred_element_type=F32)
    return wide[:, 0:width] + wide[:, width : 2 * width] + wide[:, 2 * width :]


def dot_pick(values, ones):
    rows = values.shape[0]
    tall = jnp.dot(jnp.concatenate(pieces(values), axis=0), ones.astype(BF16), preferred_element_type=F32)
    return tall[0:rows] + tall[rows : 2 * rows] + tall[2 * rows :]


def pack_tiles(weights, cells, dest, live, send, sums, nz):
    n_slab = send.shape[0]
    tiles, lanes = cells.shape
    slab = iota((n_slab, tiles), 0)
    tile = iota((n_slab, tiles), 1)
    match = jnp.where((dest[...] == slab) & (tile < live), 1.0, 0.0)
    earlier = jnp.where(iota((tiles, tiles), 0) < iota((tiles, tiles), 1), 1.0, 0.0)
    before = jnp.dot(match, earlier, preferred_element_type=F32)
    for j in range(2):
        pick = jnp.where(before == j, match, 0.0)
        for c in range(4):
            rows = weights[c] if c < 3 else (cells[...] + 1).astype(F32)
            send[:, 4 * j + c, :] = pick_dot(pick, rows)
    levels = nz // CB
    level = (cells[...] & (nz - 1)) // CB
    lane = iota((tiles, lanes), 1)
    by_level = jnp.zeros((tiles, lanes), F32)
    for l in range(levels):
        here = level == l
        for c in range(3):
            total = jnp.sum(jnp.where(here, weights[c], 0.0), axis=1, keepdims=True)
            by_level = jnp.where(lane == c * levels + l, total, by_level)
    row = iota((NEAR * 8, tiles), 0)
    member = jnp.where(row % 8 < n_slab // NEAR, row % 8 * NEAR + row // 8, -1)
    match = jnp.where((dest[...] == member) & (iota((NEAR * 8, tiles), 1) < live), 1.0, 0.0)
    added = pick_dot(match, by_level)
    sums[...] = added.reshape(NEAR, 8, lanes)


def deposit(tiles, lhs, rhs, total, first, last):
    rows, nz = total.shape[0] // 3, total.shape[1]
    width = 2 * tiles.shape[2]
    group = lhs.shape[1] // (2 * width)
    shift = nz.bit_length() - 1
    number = iota((rows, width), 0).astype(F32).astype(BF16)
    one, zero = jnp.ones((), BF16), jnp.zeros((), BF16)

    def add(i, carry):
        for g in range(group):
            tile = tiles[i * group + g]
            entry = [jnp.concatenate([tile[c : c + 1], tile[4 + c : 5 + c]], axis=1) for c in range(4)]
            cell = entry[3].astype(jnp.int32) - 1
            high = (cell >> shift).astype(F32).astype(BF16)
            low = (cell & (nz - 1)).astype(F32).astype(BF16)
            here = number == high
            at = 2 * g * width
            for c in range(3):
                first_piece = entry[c].astype(BF16)
                second_piece = (entry[c] - first_piece.astype(F32)).astype(BF16)
                lhs[c * rows : (c + 1) * rows, at : at + width] = jnp.where(here, first_piece, zero)
                lhs[c * rows : (c + 1) * rows, at + width : at + 2 * width] = jnp.where(here, second_piece, zero)
            onehot = jnp.where(number == low, one, zero)
            rhs[:, at : at + width] = onehot
            rhs[:, at + width : at + 2 * width] = onehot
        total[...] += lax.dot_general(lhs[...], rhs[...], (((1,), (1,)), ((), ())), preferred_element_type=F32)
        return carry

    lax.fori_loop(first, last, add, 0)


def step_kernel(
    n_slab, n_pencil, sigma, vort, velo, visc, weights, cells, dest, count,
    out_hbm, far,
    field, wtile, ctile, send, tiles, sums_send, sums_in, yface, yhalo, lhs, rhs, total, out, message, everywhere, beside,
    kern, partial, inbox, load_sem, xsend, xrecv, xsend2, xrecv2, ysend, yrecv, tsend, trecv, msend, mrecv, asend, arecv, bsend, brecv, ready, out_sem,
):
    slab, pencil = lax.axis_index("slab"), lax.axis_index("pencil")
    cx, cy, nz = out.shape[1], out.shape[2], out.shape[3]
    lanes = partial.shape[1]
    levels = nz // CB
    waves = [min(2 * GREET, n_slab - 1)]
    while waves[-1] < n_slab - 1:
        waves.append(min(2 * waves[-1], n_slab - 1))

    def slab_peer(i):
        return {"slab": lax.rem(slab + offset(i) + n_slab, n_slab)}

    def pencil_peer(i):
        return {"pencil": lax.rem(pencil + offset(i) + n_pencil, n_pencil)}

    loads = [
        pltpu.make_async_copy(vort, field.at[0:3, 1 : cx + 1], load_sem.at[0]),
        pltpu.make_async_copy(velo, field.at[3:6, 1 : cx + 1], load_sem.at[1]),
        pltpu.make_async_copy(visc, field.at[6, 1 : cx + 1], load_sem.at[2]),
    ]
    tile_loads = [
        pltpu.make_async_copy(weights, wtile, load_sem.at[3]),
        pltpu.make_async_copy(cells, ctile, load_sem.at[4]),
    ]
    for load in loads + tile_loads:
        load.start()
    barrier = pltpu.get_barrier_semaphore()

    def greet(where):
        pl.semaphore_signal(barrier, inc=1, device_id=where, device_id_type=MESH)

    far_first(1, waves[0], lambda i: greet(slab_peer(i)))
    far_first(1, n_pencil - 1, lambda i: greet(pencil_peer(i)))
    for load in loads:
        load.wait()
    for c in range(FIELDS):
        yface[0, c] = field[c, 1 : cx + 1, 0, :]
        yface[1, c] = field[c, 1 : cx + 1, cy - 1, :]
    pl.semaphore_wait(barrier, waves[0] + n_pencil - 1)

    s_up, s_down = slab_peer(1), slab_peer(2)
    p_up, p_down = pencil_peer(1), pencil_peer(2)
    yhalos = [
        remote(yface.at[0], yhalo.at[1], ysend.at[0], yrecv.at[1], p_down),
        remote(yface.at[1], yhalo.at[0], ysend.at[1], yrecv.at[0], p_up),
    ]
    low, high = slice(0, cy // 2), slice(cy // 2, cy)

    def face_halos(to_lower, to_upper, send_sem, recv_sem):
        return [
            remote(field.at[:, 1, to_lower], field.at[:, cx + 1, to_lower], send_sem.at[0], recv_sem.at[1], s_down),
            remote(field.at[:, cx, to_upper], field.at[:, 0, to_upper], send_sem.at[1], recv_sem.at[0], s_up),
        ]

    xhalos = face_halos(high, low, xsend, xrecv)
    xhalos2 = face_halos(low, high, xsend2, xrecv2)
    for halo in yhalos + xhalos:
        halo.start()

    def announce(step):
        for i in (waves[step] - 1, waves[step]):
            pl.semaphore_signal(ready.at[step], inc=1, device_id=slab_peer(i), device_id_type=MESH)

    def destination(i):
        return lax.rem(slab + offset(i) + n_slab, n_slab)

    def send_tiles(wave):
        first = 1 if wave == 0 else waves[wave - 1] + 1

        def one(i):
            remote(send.at[destination(i)], tiles.at[i], tsend.at[wave], trecv.at[wave], slab_peer(i)).start()

        far_first(first, waves[wave], one)

    def tiles_of(wave):
        first = 1 if wave == 0 else waves[wave - 1] + 1
        part = slice(first, waves[wave] + 1)
        return remote(send.at[part], tiles.at[part], tsend.at[wave], trecv.at[wave], s_up)

    if len(waves) > 1:
        announce(0)
    for load in tile_loads:
        load.wait()
    pack_tiles(wtile, ctile, dest, count[0], send, sums_send, nz)
    mine = lax.rem(slab, NEAR)

    def to_member(j):
        other = lax.rem(mine + j, NEAR)
        return remote(sums_send.at[other], sums_in.at[j], msend, mrecv, {"slab": slab - mine + other})

    for j in range(1, NEAR):
        to_member(j).start()
    send_tiles(0)
    tiles[0] = send[slab]
    sums_in[0] = sums_send[mine]
    total[...] = jnp.zeros_like(total)
    beside[...] = jnp.zeros_like(beside)
    for step in range(1, len(waves) - 1):
        pl.semaphore_wait(ready.at[step - 1], 2)
        announce(step)
        send_tiles(step)
    for halo in yhalos:
        halo.wait()

    row = iota((cy, nz), 0)
    first_row, last_row = row == 0, row == cy - 1
    has_before, has_after = pencil > 0, pencil < n_pencil - 1

    def plane(x, sums, is_first=False, is_last=False):
        def ahead_y(c):
            edge = jnp.where(has_after, yhalo[1, c, pl.ds(x, 1), :], 0.0)
            return jnp.where(last_row, edge, pltpu.roll(field[c, x + 1], cy - 1, 0))

        def behind_y(c):
            edge = jnp.where(has_before, yhalo[0, c, pl.ds(x, 1), :], 0.0)
            return jnp.where(first_row, edge, pltpu.roll(field[c, x + 1], 1, 0))

        neighbours = [
            (
                (lambda c: 0.0) if is_last else (lambda c: field[c, x + 2]),
                (lambda c: 0.0) if is_first else (lambda c: field[c, x]),
            ),
            (ahead_y, behind_y),
            (lambda c: pltpu.roll(field[c, x + 1], nz - 1, 1), lambda c: pltpu.roll(field[c, x + 1], 1, 1)),
        ]
        own = [field[c, x + 1] for c in range(3)]
        own_visc = field[6, x + 1]
        change = [jnp.zeros_like(own_visc) for c in range(3)]
        for d, (forward, backward) in enumerate(neighbours):
            factor = 0.5 * own[d]
            face_ahead = 0.5 * (own_visc + forward(6))
            face_behind = 0.5 * (own_visc + backward(6))
            for c in range(3):
                change[c] += factor * (forward(3 + c) - backward(3 + c))
                if d > 0 or not is_last:
                    change[c] += face_ahead * (forward(c) - own[c])
                if d > 0 or not is_first:
                    change[c] += face_behind * (backward(c) - own[c])
        result = []
        for c in range(3):
            value = own[c] + time_step * change[c]
            out[c, x] = value
            result.append(sums[c] + jnp.sum(value, axis=0, keepdims=True))
        return tuple(result)

    def face(inner, outer, exists, sign, rows):
        here = [field[c, inner, rows] for c in range(FIELDS)]
        there = [jnp.where(exists, field[c, outer, rows], 0.0) for c in range(FIELDS)]
        middle = 0.5 * (here[6] + there[6])
        for_here, for_there = [], []
        for c in range(3):
            flow = middle * (there[c] - here[c])
            for_here.append(time_step * (sign * (0.5 * here[0]) * there[3 + c] + flow))
            for_there.append(jnp.where(exists, time_step * (-sign * (0.5 * there[0]) * here[3 + c] - flow), 0.0))
        return for_here, for_there

    def rim(inner, exists, rows):
        viscous = 0.5 * time_step * field[6, inner, rows]
        return [jnp.where(exists, 0.0, -viscous * field[c, inner, rows]) for c in range(3)]

    def over_rows(values):
        return [jnp.sum(value, axis=0, keepdims=True) for value in values]

    sums = lax.fori_loop(1, SPLIT, plane, tuple(jnp.zeros((1, nz), F32) for c in range(3)))
    if len(waves) > 1:
        pl.semaphore_wait(ready.at[len(waves) - 2], 2)
        send_tiles(len(waves) - 1)
    sums = lax.fori_loop(SPLIT, cx - 1, plane, sums)
    sums = plane(0, sums, is_first=True)
    sums = plane(cx - 1, sums, is_last=True)
    has_lower, has_upper = slab > 0, slab < n_slab - 1
    rims = [over_rows(rim(1, has_lower, high)), over_rows(rim(cx, has_upper, low))]
    sums = [sums[c] + rims[0][c] + rims[1][c] for c in range(3)]
    for halo in xhalos:
        halo.wait()
    lower_own, lower_other = map(over_rows, face(1, 0, has_lower, -1.0, low))
    upper_own, upper_other = map(over_rows, face(cx, cx + 1, has_upper, 1.0, high))
    sums = [sums[c] + lower_own[c] + upper_own[c] for c in range(3)]
    width = sums_in.shape[2]
    group = jnp.where(iota((nz, width), 0) // CB == iota((nz, width), 1) % levels, 1.0, 0.0)
    stacked = jnp.concatenate(sums + upper_other + lower_other + [jnp.zeros((7, nz), F32)], axis=0)
    spread = dot_pick(stacked, group)
    sublane, lane = iota((16, width), 0), iota((16, width), 1)
    part, third = lane // levels % 4, lane // (width // 2)

    def line(mask):
        return jnp.sum(jnp.where(mask, spread, 0.0), axis=0, keepdims=True)

    own_line = line((third == 0) & (part < 3) & (sublane == part))
    beside_line = line((part < 3) & (sublane == 3 + 3 * third + part))
    all_sums = remote(sums_send.at[1:NEAR], sums_in.at[1:NEAR], msend, mrecv, s_up)
    all_sums.wait_recv()
    rows = jnp.sum(sums_in[...], axis=0) + jnp.where(iota((8, width), 0) == slab // NEAR, own_line, 0.0)
    message[0:4] = rows[0:4] + pltpu.roll(rows, width // 2, 1)[4:8]
    message[4:5] = beside_line
    far_first(
        1, n_slab - 1,
        lambda i: remote(message.at[0:5], everywhere.at[slab, 0:5], bsend, brecv, slab_peer(i)).start(),
    )
    for halo in xhalos2:
        halo.start()
    everywhere[slab, 0:5] = message[0:5]
    gathered = remote(everywhere.at[1:n_slab, 0:5], everywhere.at[1:n_slab, 0:5], bsend, brecv, s_up)

    shape = (8, lanes)
    rel_x = [((slab - iota(shape, 0) * NEAR - x) * cx).astype(F32) for x in range(NEAR)]
    rel_y = ((iota(shape, 1) // levels - pencil) * cy).astype(F32)
    target_level = iota(shape, 1) % levels

    def rel_z(level):
        return ((target_level - level) * CB).astype(F32)

    def prepare(level, carry):
        along_z = rel_z(level)
        flat_sq = rel_y * rel_y + along_z * along_z + sigma * sigma
        for x in range(NEAR):
            inverse = lax.rsqrt(rel_x[x] * rel_x[x] + flat_sq)
            kern[level * NEAR + x] = inverse * inverse * inverse
        return carry

    lax.fori_loop(0, levels, prepare, 0)
    groups = tiles.shape[0] * 4 * tiles.shape[2] // lhs.shape[1]
    early = max(1, len(waves) - 1)
    for wave in range(early):
        tiles_of(wave).wait_recv()
    deposit(tiles, lhs, rhs, total, 0, groups // 2)
    for wave in range(early, len(waves)):
        tiles_of(wave).wait_recv()
    cut = groups * BEFORE // 8
    deposit(tiles, lhs, rhs, total, groups // 2, cut)

    gathered.wait_recv()
    beside[8 : 8 + n_slab, :] = everywhere[:, 4, :]
    moments = []
    for x in range(NEAR):
        rows = everywhere[x, 0:4]
        for z in range(1, n_slab // NEAR):
            rows = rows + everywhere[z * NEAR + x, 0:4]
        rows = jnp.concatenate([rows, pltpu.roll(rows, width // 2, 1)], axis=0)
        from_lower = beside[pl.ds(7 + x, 8, stride=NEAR), :]
        from_upper = beside[pl.ds(9 + x, 8, stride=NEAR), :]
        moments.append(rows + from_lower + pltpu.roll(from_upper, width // 2, 1))
    sums = [jnp.zeros(shape, F32) for c in range(3)]
    for level in range(levels):
        along_z = rel_z(level)
        for x in range(NEAR):
            m0, m1, m2 = (moments[x][:, c * levels + level : c * levels + level + 1] for c in range(3))
            weight = kern[level * NEAR + x]
            sums[0] += weight * (along_z * m1 - rel_y * m2)
            sums[1] += weight * (rel_x[x] * m2 - along_z * m0)
            sums[2] += weight * (rel_y * m0 - rel_x[x] * m1)
    lines = [jnp.sum(part, axis=0, keepdims=True) for part in sums]
    partial[0:4] = jnp.concatenate(lines + [jnp.zeros((1, lanes), F32)], axis=0)
    far_first(1, n_pencil - 1, lambda i: remote(partial.at[0:4], inbox.at[i, 0:4], asend, arecv, pencil_peer(i)).start())
    inbox[0, 0:4] = partial[0:4]
    arrived = remote(inbox.at[1:n_pencil, 0:4], inbox.at[1:n_pencil, 0:4], asend, arecv, p_up)

    deposit(tiles, lhs, rhs, total, cut, groups)
    for halo in xhalos2:
        halo.wait()
    everything = slice(0, cy)
    for x, inner, outer, exists, sign in ((0, 1, 0, has_lower, -1.0), (cx - 1, cx, cx + 1, has_upper, 1.0)):
        terms, _ = face(inner, outer, exists, sign, everything)
        for c in range(3):
            out[c, x] += terms[c]
    stores = [pltpu.make_async_copy(out.at[c], out_hbm.at[c], out_sem.at[c]) for c in range(3)]
    for c in range(3):
        out[c] += total[c * cx * cy : (c + 1) * cx * cy].reshape(cx, cy, nz)
        stores[c].start()
    arrived.wait_recv()
    result = pltpu.roll(jnp.sum(inbox[:, 0:4, :], axis=0), lax.rem(lanes - pencil * levels, lanes), 1)
    for c in range(3):
        far[c, 0] = result[c : c + 1, 0:levels]
    all_sums.wait_send()
    for wave in range(len(waves)):
        tiles_of(wave).wait_send()
    arrived.wait_send()
    gathered.wait_send()
    for store in stores:
        store.wait()


BEFORE = 5
NEAR = 4
GREET = 4
SPLIT = 4
GROUP = 4


def per_device(n_slab, n_pencil, vorticity, velocity, viscosity, tile_weights, tile_cells, tile_dest, tile_count):
    _, cx, cy, nz = vorticity.shape
    n_tiles, tile_len = tile_cells.shape
    levels = nz // CB
    lanes = n_pencil * levels
    hbm = pl.BlockSpec(memory_space=pltpu.HBM)
    vmem = pl.BlockSpec(memory_space=pltpu.VMEM)
    smem = pl.BlockSpec(memory_space=pltpu.SMEM)
    dma = pltpu.SemaphoreType.DMA
    outs = (jax.ShapeDtypeStruct(vorticity.shape, F32), jax.ShapeDtypeStruct((3, 1, 1, levels), F32))
    return pl.pallas_call(
        functools.partial(step_kernel, n_slab, n_pencil, float(cx * n_slab // 4)),
        out_shape=outs,
        in_specs=[hbm, hbm, hbm, hbm, hbm, vmem, smem],
        out_specs=(hbm, vmem),
        scratch_shapes=[
            pltpu.VMEM((FIELDS, cx + 2, cy, nz), F32),
            pltpu.VMEM((3, n_tiles, tile_len), F32),
            pltpu.VMEM((n_tiles, tile_len), jnp.int32),
            pltpu.VMEM((n_slab, 8, tile_len), F32),
            pltpu.VMEM((n_slab, 8, tile_len), F32),
            pltpu.VMEM((NEAR, 8, tile_len), F32),
            pltpu.VMEM((NEAR, 8, tile_len), F32),
            pltpu.VMEM((2, FIELDS, cx, nz), F32),
            pltpu.VMEM((2, FIELDS, cx, nz), F32),
            pltpu.VMEM((3 * cx * cy, GROUP * 4 * tile_len), BF16),
            pltpu.VMEM((nz, GROUP * 4 * tile_len), BF16),
            pltpu.VMEM((3 * cx * cy, nz), F32),
            pltpu.VMEM((3, cx, cy, nz), F32),
            pltpu.VMEM((8, tile_len), F32),
            pltpu.VMEM((n_slab, 8, tile_len), F32),
            pltpu.VMEM((8 * NEAR + 16, tile_len), F32),
            pltpu.VMEM((levels * NEAR, 8, lanes), F32),
            pltpu.VMEM((8, lanes), F32),
            pltpu.VMEM((n_pencil, 8, lanes), F32),
            dma((5,)), dma((2,)), dma((2,)), dma((2,)), dma((2,)), dma((2,)), dma((2,)), dma((4,)), dma((4,)), dma, dma, dma, dma, dma, dma,
            pltpu.SemaphoreType.REGULAR((4,)), dma((3,)),
        ],
        compiler_params=pltpu.CompilerParams(collective_id=0, has_side_effects=True, vmem_limit_bytes=VMEM_LIMIT),
        name="step",
    )(
        vorticity, velocity, viscosity, jnp.transpose(tile_weights, (1, 0, 2)), tile_cells,
        tile_dest.reshape(1, -1), tile_count,
    )


def solution(mesh):
    in_specs = (
        P(None, "slab", "pencil", None),
        P(None, "slab", "pencil", None),
        P("slab", "pencil", None),
        P(("slab", "pencil"), None, None),
        P(("slab", "pencil"), None),
        P(("slab", "pencil"), None),
        P(("slab", "pencil")),
    )
    out_specs = (P(None, "slab", "pencil", None), P(None, "slab", "pencil", None))
    step = functools.partial(per_device, mesh.shape["slab"], mesh.shape["pencil"])
    return jax.shard_map(step, mesh=mesh, in_specs=in_specs, out_specs=out_specs, check_vma=False)
```

```python
import functools

import jax
import jax.numpy as jnp
from jax import lax
from jax.experimental import pallas as pl
from jax.experimental.pallas import tpu as pltpu
from jax.sharding import PartitionSpec as P

CB = 16
FIELDS = 7
time_step = 0.1
VMEM_LIMIT = 60 << 20
HIGH = lax.Precision.HIGHEST
F32 = jnp.float32
BF16 = jnp.bfloat16
MESH = pl.DeviceIdType.MESH


def iota(shape, dim):
    return lax.broadcasted_iota(jnp.int32, shape, dim)


def offset(i):
    return (2 * (i % 2) - 1) * ((i + 1) // 2)


def far_first(first, last, one):
    def body(j, carry):
        one(last - j)
        return carry

    lax.fori_loop(0, last - first + 1, body, 0)


def remote(src, dst, send_sem, recv_sem, device):
    return pltpu.make_async_remote_copy(
        src_ref=src, dst_ref=dst, send_sem=send_sem, recv_sem=recv_sem, device_id=device, device_id_type=MESH
    )


def pieces(values):
    first = values.astype(BF16)
    rest = values - first.astype(F32)
    second = rest.astype(BF16)
    return [first, second, (rest - second.astype(F32)).astype(BF16)]


def pick_dot(ones, values):
    width = values.shape[1]
    wide = jnp.dot(ones.astype(BF16), jnp.concatenate(pieces(values), axis=1), preferred_element_type=F32)
    return wide[:, 0:width] + wide[:, width : 2 * width] + wide[:, 2 * width :]


def dot_pick(values, ones):
    rows = values.shape[0]
    tall = jnp.dot(jnp.concatenate(pieces(values), axis=0), ones.astype(BF16), preferred_element_type=F32)
    return tall[0:rows] + tall[rows : 2 * rows] + tall[2 * rows :]


def pack_tiles(weights, cells, dest, live, send, sums, nz):
    n_slab = send.shape[0]
    tiles, lanes = cells.shape
    slab = iota((n_slab, tiles), 0)
    tile = iota((n_slab, tiles), 1)
    match = jnp.where((dest[...] == slab) & (tile < live), 1.0, 0.0)
    earlier = jnp.where(iota((tiles, tiles), 0) < iota((tiles, tiles), 1), 1.0, 0.0)
    before = jnp.dot(match, earlier, preferred_element_type=F32)
    for j in range(2):
        pick = jnp.where(before == j, match, 0.0)
        for c in range(4):
            rows = weights[c] if c < 3 else (cells[...] + 1).astype(F32)
            send[:, 4 * j + c, :] = pick_dot(pick, rows)
    levels = nz // CB
    level = (cells[...] & (nz - 1)) // CB
    lane = iota((tiles, lanes), 1)
    by_level = jnp.zeros((tiles, lanes), F32)
    for l in range(levels):
        here = level == l
        for c in range(3):
            total = jnp.sum(jnp.where(here, weights[c], 0.0), axis=1, keepdims=True)
            by_level = jnp.where(lane == c * levels + l, total, by_level)
    row = iota((NEAR * 8, tiles), 0)
    member = jnp.where(row % 8 < n_slab // NEAR, row % 8 * NEAR + row // 8, -1)
    match = jnp.where((dest[...] == member) & (iota((NEAR * 8, tiles), 1) < live), 1.0, 0.0)
    added = pick_dot(match, by_level)
    sums[...] = added.reshape(NEAR, 8, lanes)


def deposit(tiles, lhs, rhs, total, first, last):
    rows, nz = total.shape[0] // 3, total.shape[1]
    width = 2 * tiles.shape[2]
    group = lhs.shape[1] // (2 * width)
    shift = nz.bit_length() - 1
    number = iota((rows, width), 0).astype(F32).astype(BF16)
    one, zero = jnp.ones((), BF16), jnp.zeros((), BF16)

    def add(i, carry):
        for g in range(group):
            tile = tiles[i * group + g]
            entry = [jnp.concatenate([tile[c : c + 1], tile[4 + c : 5 + c]], axis=1) for c in range(4)]
            cell = entry[3].astype(jnp.int32) - 1
            high = (cell >> shift).astype(F32).astype(BF16)
            low = (cell & (nz - 1)).astype(F32).astype(BF16)
            here = number == high
            at = 2 * g * width
            for c in range(3):
                first_piece = entry[c].astype(BF16)
                second_piece = (entry[c] - first_piece.astype(F32)).astype(BF16)
                lhs[c * rows : (c + 1) * rows, at : at + width] = jnp.where(here, first_piece, zero)
                lhs[c * rows : (c + 1) * rows, at + width : at + 2 * width] = jnp.where(here, second_piece, zero)
            onehot = jnp.where(number == low, one, zero)
            rhs[:, at : at + width] = onehot
            rhs[:, at + width : at + 2 * width] = onehot
        total[...] += lax.dot_general(lhs[...], rhs[...], (((1,), (1,)), ((), ())), preferred_element_type=F32)
        return carry

    lax.fori_loop(first, last, add, 0)


def step_kernel(
    n_slab, n_pencil, sigma, vort, velo, visc, weights, cells, dest, count,
    out_hbm, far,
    field, wtile, ctile, send, tiles, sums_send, sums_in, yface, yhalo, lhs, rhs, total, out, message, everywhere, beside,
    kern, partial, inbox, load_sem, xsend, xrecv, xsend2, xrecv2, ysend, yrecv, tsend, trecv, msend, mrecv, asend, arecv, bsend, brecv, ready, out_sem,
):
    slab, pencil = lax.axis_index("slab"), lax.axis_index("pencil")
    cx, cy, nz = out.shape[1], out.shape[2], out.shape[3]
    lanes = partial.shape[1]
    levels = nz // CB
    waves = [min(2 * GREET, n_slab - 1)]
    while waves[-1] < n_slab - 1:
        waves.append(min(2 * waves[-1], n_slab - 1))

    def slab_peer(i):
        return {"slab": lax.rem(slab + offset(i) + n_slab, n_slab)}

    def pencil_peer(i):
        return {"pencil": lax.rem(pencil + offset(i) + n_pencil, n_pencil)}

    loads = [
        pltpu.make_async_copy(vort, field.at[0:3, 1 : cx + 1], load_sem.at[0]),
        pltpu.make_async_copy(velo, field.at[3:6, 1 : cx + 1], load_sem.at[1]),
        pltpu.make_async_copy(visc, field.at[6, 1 : cx + 1], load_sem.at[2]),
    ]
    tile_loads = [
        pltpu.make_async_copy(weights, wtile, load_sem.at[3]),
        pltpu.make_async_copy(cells, ctile, load_sem.at[4]),
    ]
    barrier = pltpu.get_barrier_semaphore()

    def greet(where):
        pl.semaphore_signal(barrier, inc=1, device_id=where, device_id_type=MESH)

    far_first(1, waves[0], lambda i: greet(slab_peer(i)))
    far_first(1, n_pencil - 1, lambda i: greet(pencil_peer(i)))
    for load in loads + tile_loads:
        load.start()
    for load in loads:
        load.wait()
    for c in range(FIELDS):
        yface[0, c] = field[c, 1 : cx + 1, 0, :]
        yface[1, c] = field[c, 1 : cx + 1, cy - 1, :]
    pl.semaphore_wait(barrier, waves[0] + n_pencil - 1)

    s_up, s_down = slab_peer(1), slab_peer(2)
    p_up, p_down = pencil_peer(1), pencil_peer(2)
    yhalos = [
        remote(yface.at[0], yhalo.at[1], ysend.at[0], yrecv.at[1], p_down),
        remote(yface.at[1], yhalo.at[0], ysend.at[1], yrecv.at[0], p_up),
    ]
    low, high = slice(0, cy // 2), slice(cy // 2, cy)

    def face_halos(to_lower, to_upper, send_sem, recv_sem):
        return [
            remote(field.at[:, 1, to_lower], field.at[:, cx + 1, to_lower], send_sem.at[0], recv_sem.at[1], s_down),
            remote(field.at[:, cx, to_upper], field.at[:, 0, to_upper], send_sem.at[1], recv_sem.at[0], s_up),
        ]

    xhalos = face_halos(high, low, xsend, xrecv)
    xhalos2 = face_halos(low, high, xsend2, xrecv2)
    for halo in yhalos + xhalos:
        halo.start()

    def announce(step):
        for i in (waves[step] - 1, waves[step]):
            pl.semaphore_signal(ready.at[step], inc=1, device_id=slab_peer(i), device_id_type=MESH)

    def destination(i):
        return lax.rem(slab + offset(i) + n_slab, n_slab)

    def send_tiles(wave):
        first = 1 if wave == 0 else waves[wave - 1] + 1

        def one(i):
            remote(send.at[destination(i)], tiles.at[i], tsend.at[wave], trecv.at[wave], slab_peer(i)).start()

        far_first(first, waves[wave], one)

    def tiles_of(wave):
        first = 1 if wave == 0 else waves[wave - 1] + 1
        part = slice(first, waves[wave] + 1)
        return remote(send.at[part], tiles.at[part], tsend.at[wave], trecv.at[wave], s_up)

    if len(waves) > 1:
        announce(0)
    for load in tile_loads:
        load.wait()
    pack_tiles(wtile, ctile, dest, count[0], send, sums_send, nz)
    mine = lax.rem(slab, NEAR)

    def to_member(j):
        other = lax.rem(mine + j, NEAR)
        return remote(sums_send.at[other], sums_in.at[j], msend, mrecv, {"slab": slab - mine + other})

    for j in range(1, NEAR):
        to_member(j).start()
    send_tiles(0)
    tiles[0] = send[slab]
    sums_in[0] = sums_send[mine]
    total[...] = jnp.zeros_like(total)
    beside[...] = jnp.zeros_like(beside)
    for step in range(1, len(waves) - 1):
        pl.semaphore_wait(ready.at[step - 1], 2)
        announce(step)
        send_tiles(step)
    for halo in yhalos:
        halo.wait()

    row = iota((cy, nz), 0)
    first_row, last_row = row == 0, row == cy - 1
    has_before, has_after = pencil > 0, pencil < n_pencil - 1

    def plane(x, sums, is_first=False, is_last=False):
        def ahead_y(c):
            edge = jnp.where(has_after, yhalo[1, c, pl.ds(x, 1), :], 0.0)
            return jnp.where(last_row, edge, pltpu.roll(field[c, x + 1], cy - 1, 0))

        def behind_y(c):
            edge = jnp.where(has_before, yhalo[0, c, pl.ds(x, 1), :], 0.0)
            return jnp.where(first_row, edge, pltpu.roll(field[c, x + 1], 1, 0))

        neighbours = [
            (
                (lambda c: 0.0) if is_last else (lambda c: field[c, x + 2]),
                (lambda c: 0.0) if is_first else (lambda c: field[c, x]),
            ),
            (ahead_y, behind_y),
            (lambda c: pltpu.roll(field[c, x + 1], nz - 1, 1), lambda c: pltpu.roll(field[c, x + 1], 1, 1)),
        ]
        own = [field[c, x + 1] for c in range(3)]
        own_visc = field[6, x + 1]
        change = [jnp.zeros_like(own_visc) for c in range(3)]
        for d, (forward, backward) in enumerate(neighbours):
            factor = 0.5 * own[d]
            face_ahead = 0.5 * (own_visc + forward(6))
            face_behind = 0.5 * (own_visc + backward(6))
            for c in range(3):
                change[c] += factor * (forward(3 + c) - backward(3 + c))
                if d > 0 or not is_last:
                    change[c] += face_ahead * (forward(c) - own[c])
                if d > 0 or not is_first:
                    change[c] += face_behind * (backward(c) - own[c])
        result = []
        for c in range(3):
            value = own[c] + time_step * change[c]
            out[c, x] = value
            result.append(sums[c] + jnp.sum(value, axis=0, keepdims=True))
        return tuple(result)

    def face(inner, outer, exists, sign, rows):
        here = [field[c, inner, rows] for c in range(FIELDS)]
        there = [jnp.where(exists, field[c, outer, rows], 0.0) for c in range(FIELDS)]
        middle = 0.5 * (here[6] + there[6])
        for_here, for_there = [], []
        for c in range(3):
            flow = middle * (there[c] - here[c])
            for_here.append(time_step * (sign * (0.5 * here[0]) * there[3 + c] + flow))
            for_there.append(jnp.where(exists, time_step * (-sign * (0.5 * there[0]) * here[3 + c] - flow), 0.0))
        return for_here, for_there

    def rim(inner, exists, rows):
        viscous = 0.5 * time_step * field[6, inner, rows]
        return [jnp.where(exists, 0.0, -viscous * field[c, inner, rows]) for c in range(3)]

    def over_rows(values):
        return [jnp.sum(value, axis=0, keepdims=True) for value in values]

    sums = lax.fori_loop(1, SPLIT, plane, tuple(jnp.zeros((1, nz), F32) for c in range(3)))
    if len(waves) > 1:
        pl.semaphore_wait(ready.at[len(waves) - 2], 2)
        send_tiles(len(waves) - 1)
    sums = lax.fori_loop(SPLIT, cx - 1, plane, sums)
    sums = plane(0, sums, is_first=True)
    sums = plane(cx - 1, sums, is_last=True)
    has_lower, has_upper = slab > 0, slab < n_slab - 1
    rims = [over_rows(rim(1, has_lower, high)), over_rows(rim(cx, has_upper, low))]
    sums = [sums[c] + rims[0][c] + rims[1][c] for c in range(3)]
    for halo in xhalos:
        halo.wait()
    lower_own, lower_other = map(over_rows, face(1, 0, has_lower, -1.0, low))
    upper_own, upper_other = map(over_rows, face(cx, cx + 1, has_upper, 1.0, high))
    sums = [sums[c] + lower_own[c] + upper_own[c] for c in range(3)]
    width = sums_in.shape[2]
    group = jnp.where(iota((nz, width), 0) // CB == iota((nz, width), 1) % levels, 1.0, 0.0)
    stacked = jnp.concatenate(sums + upper_other + lower_other + [jnp.zeros((7, nz), F32)], axis=0)
    spread = dot_pick(stacked, group)
    sublane, lane = iota((16, width), 0), iota((16, width), 1)
    part, third = lane // levels % 4, lane // (width // 2)

    def line(mask):
        return jnp.sum(jnp.where(mask, spread, 0.0), axis=0, keepdims=True)

    own_line = line((third == 0) & (part < 3) & (sublane == part))
    beside_line = line((part < 3) & (sublane == 3 + 3 * third + part))
    all_sums = remote(sums_send.at[1:NEAR], sums_in.at[1:NEAR], msend, mrecv, s_up)
    all_sums.wait_recv()
    rows = jnp.sum(sums_in[...], axis=0) + jnp.where(iota((8, width), 0) == slab // NEAR, own_line, 0.0)
    message[0:4] = rows[0:4] + pltpu.roll(rows, width // 2, 1)[4:8]
    message[4:5] = beside_line
    far_first(
        1, n_slab - 1,
        lambda i: remote(message.at[0:5], everywhere.at[slab, 0:5], bsend, brecv, slab_peer(i)).start(),
    )
    for halo in xhalos2:
        halo.start()
    everywhere[slab, 0:5] = message[0:5]
    gathered = remote(everywhere.at[1:n_slab, 0:5], everywhere.at[1:n_slab, 0:5], bsend, brecv, s_up)

    shape = (8, lanes)
    rel_x = [((slab - iota(shape, 0) * NEAR - x) * cx).astype(F32) for x in range(NEAR)]
    rel_y = ((iota(shape, 1) // levels - pencil) * cy).astype(F32)
    target_level = iota(shape, 1) % levels

    def rel_z(level):
        return ((target_level - level) * CB).astype(F32)

    def prepare(level, carry):
        along_z = rel_z(level)
        flat_sq = rel_y * rel_y + along_z * along_z + sigma * sigma
        for x in range(NEAR):
            inverse = lax.rsqrt(rel_x[x] * rel_x[x] + flat_sq)
            kern[level * NEAR + x] = inverse * inverse * inverse
        return carry

    lax.fori_loop(0, levels, prepare, 0)
    groups = tiles.shape[0] * 4 * tiles.shape[2] // lhs.shape[1]
    early = max(1, len(waves) - 1)
    for wave in range(early):
        tiles_of(wave).wait_recv()
    deposit(tiles, lhs, rhs, total, 0, groups // 2)
    for wave in range(early, len(waves)):
        tiles_of(wave).wait_recv()
    cut = groups * BEFORE // 8
    deposit(tiles, lhs, rhs, total, groups // 2, cut)

    gathered.wait_recv()
    beside[8 : 8 + n_slab, :] = everywhere[:, 4, :]
    moments = []
    for x in range(NEAR):
        rows = everywhere[x, 0:4]
        for z in range(1, n_slab // NEAR):
            rows = rows + everywhere[z * NEAR + x, 0:4]
        rows = jnp.concatenate([rows, pltpu.roll(rows, width // 2, 1)], axis=0)
        from_lower = beside[pl.ds(7 + x, 8, stride=NEAR), :]
        from_upper = beside[pl.ds(9 + x, 8, stride=NEAR), :]
        moments.append(rows + from_lower + pltpu.roll(from_upper, width // 2, 1))
    sums = [jnp.zeros(shape, F32) for c in range(3)]
    for level in range(levels):
        along_z = rel_z(level)
        for x in range(NEAR):
            m0, m1, m2 = (moments[x][:, c * levels + level : c * levels + level + 1] for c in range(3))
            weight = kern[level * NEAR + x]
            sums[0] += weight * (along_z * m1 - rel_y * m2)
            sums[1] += weight * (rel_x[x] * m2 - along_z * m0)
            sums[2] += weight * (rel_y * m0 - rel_x[x] * m1)
    lines = [jnp.sum(part, axis=0, keepdims=True) for part in sums]
    partial[0:4] = jnp.concatenate(lines + [jnp.zeros((1, lanes), F32)], axis=0)
    far_first(1, n_pencil - 1, lambda i: remote(partial.at[0:4], inbox.at[i, 0:4], asend, arecv, pencil_peer(i)).start())
    inbox[0, 0:4] = partial[0:4]
    arrived = remote(inbox.at[1:n_pencil, 0:4], inbox.at[1:n_pencil, 0:4], asend, arecv, p_up)

    deposit(tiles, lhs, rhs, total, cut, groups)
    for halo in xhalos2:
        halo.wait()
    everything = slice(0, cy)
    for x, inner, outer, exists, sign in ((0, 1, 0, has_lower, -1.0), (cx - 1, cx, cx + 1, has_upper, 1.0)):
        terms, _ = face(inner, outer, exists, sign, everything)
        for c in range(3):
            out[c, x] += terms[c]
    stores = [pltpu.make_async_copy(out.at[c], out_hbm.at[c], out_sem.at[c]) for c in range(3)]
    for c in range(3):
        out[c] += total[c * cx * cy : (c + 1) * cx * cy].reshape(cx, cy, nz)
        stores[c].start()
    arrived.wait_recv()
    result = pltpu.roll(jnp.sum(inbox[:, 0:4, :], axis=0), lax.rem(lanes - pencil * levels, lanes), 1)
    for c in range(3):
        far[c, 0] = result[c : c + 1, 0:levels]
    all_sums.wait_send()
    for wave in range(len(waves)):
        tiles_of(wave).wait_send()
    arrived.wait_send()
    gathered.wait_send()
    for store in stores:
        store.wait()


BEFORE = 5
NEAR = 4
GREET = 4
SPLIT = 4
GROUP = 4


def per_device(n_slab, n_pencil, vorticity, velocity, viscosity, tile_weights, tile_cells, tile_dest, tile_count):
    _, cx, cy, nz = vorticity.shape
    n_tiles, tile_len = tile_cells.shape
    levels = nz // CB
    lanes = n_pencil * levels
    hbm = pl.BlockSpec(memory_space=pltpu.HBM)
    vmem = pl.BlockSpec(memory_space=pltpu.VMEM)
    smem = pl.BlockSpec(memory_space=pltpu.SMEM)
    dma = pltpu.SemaphoreType.DMA
    outs = (jax.ShapeDtypeStruct(vorticity.shape, F32), jax.ShapeDtypeStruct((3, 1, 1, levels), F32))
    return pl.pallas_call(
        functools.partial(step_kernel, n_slab, n_pencil, float(cx * n_slab // 4)),
        out_shape=outs,
        in_specs=[hbm, hbm, hbm, hbm, hbm, vmem, smem],
        out_specs=(hbm, vmem),
        scratch_shapes=[
            pltpu.VMEM((FIELDS, cx + 2, cy, nz), F32),
            pltpu.VMEM((3, n_tiles, tile_len), F32),
            pltpu.VMEM((n_tiles, tile_len), jnp.int32),
            pltpu.VMEM((n_slab, 8, tile_len), F32),
            pltpu.VMEM((n_slab, 8, tile_len), F32),
            pltpu.VMEM((NEAR, 8, tile_len), F32),
            pltpu.VMEM((NEAR, 8, tile_len), F32),
            pltpu.VMEM((2, FIELDS, cx, nz), F32),
            pltpu.VMEM((2, FIELDS, cx, nz), F32),
            pltpu.VMEM((3 * cx * cy, GROUP * 4 * tile_len), BF16),
            pltpu.VMEM((nz, GROUP * 4 * tile_len), BF16),
            pltpu.VMEM((3 * cx * cy, nz), F32),
            pltpu.VMEM((3, cx, cy, nz), F32),
            pltpu.VMEM((8, tile_len), F32),
            pltpu.VMEM((n_slab, 8, tile_len), F32),
            pltpu.VMEM((8 * NEAR + 16, tile_len), F32),
            pltpu.VMEM((levels * NEAR, 8, lanes), F32),
            pltpu.VMEM((8, lanes), F32),
            pltpu.VMEM((n_pencil, 8, lanes), F32),
            dma((5,)), dma((2,)), dma((2,)), dma((2,)), dma((2,)), dma((2,)), dma((2,)), dma((4,)), dma((4,)), dma, dma, dma, dma, dma, dma,
            pltpu.SemaphoreType.REGULAR((4,)), dma((3,)),
        ],
        compiler_params=pltpu.CompilerParams(collective_id=0, has_side_effects=True, vmem_limit_bytes=VMEM_LIMIT),
        name="step",
    )(
        vorticity, velocity, viscosity, jnp.transpose(tile_weights, (1, 0, 2)), tile_cells,
        tile_dest.reshape(1, -1), tile_count,
    )


def solution(mesh):
    in_specs = (
        P(None, "slab", "pencil", None),
        P(None, "slab", "pencil", None),
        P("slab", "pencil", None),
        P(("slab", "pencil"), None, None),
        P(("slab", "pencil"), None),
        P(("slab", "pencil"), None),
        P(("slab", "pencil")),
    )
    out_specs = (P(None, "slab", "pencil", None), P(None, "slab", "pencil", None))
    step = functools.partial(per_device, mesh.shape["slab"], mesh.shape["pencil"])
    return jax.shard_map(step, mesh=mesh, in_specs=in_specs, out_specs=out_specs, check_vma=False)
```
